32 devices in a mesh: node: 4 (over y, x), table: 8 (over z, core).
Axes of the slice: x: 2, y: 2, z: 4, core: 2. Of those that a mesh axis runs over, the one named last changes fastest.
Arguments:
- emb_rows: bfloat16 [16384, 128], P(('node', 'table')), may hold values from -0.23925781 to 0.23925781
- tile_mult: int32 [256, 128, 128], P(('node', 'table')), may hold values from 0 to 3
- tile_rows: int32 [256], P(('node', 'table')), may hold values from 0 to 3
- tile_table: int32 [256], P(('node', 'table')), may hold values from 0 to 7, as said below
- tile_slot: int32 [256], P(('node', 'table')), may hold values from 0 to 51
- dense: bfloat16 [8192, 128], P(('node', 'table')), may hold values from -6 to 6
- cross_v: bfloat16 [3456, 512], P('node'), may hold values from -0.109375 to 0.109375
- cross_u: bfloat16 [512, 3456], P('node'), may hold values from -0.25 to 0.25
- cross_bias: float32 [3456], replicated, may hold values from -3 to 3
- cotangent: bfloat16 [8192, 3456], P(('node', 'table')), may hold values from -0.1796875 to 0.1796875
Outputs:
- cross_out: bfloat16 [8192, 3456], P(('node', 'table'))
- emb_grad: float32 [16384, 128], P(('node', 'table'))
The draws below stay inside these ranges and needn't reach their ends.
Inputs may be any that keep to these rules, and one draw needn't show every extreme that they name: For each node index n and table index t, take the tiles j with j // 2 == n on the 4 devices of table index t: no tile_table value occurs more than 3 times among them, and the tiles with one value carry at most 2 distinct tile_slot values. Both bounds are reached in every such set.
All inputs are finite; a program needn't handle non-finite values.
Results may differ from the reference program's by a relative error of at most 0.0057.
Values may be sent and summed in bfloat16 or wider, within the bound.
No kernel may reach another device: no remote copies, remote signals or barrier semaphores. Data moves between devices by JAX's collectives and lax.ppermute only.
A program may use at most 128 MiB of HBM per device.

```python
import jax
import jax.numpy as jnp
from jax import lax

EMB = 128
FEATURES = 26
RANK = 512
BLOCK = 128
SAMP_DEV = 256
ROW_BLOCKS = 4
TILE_LIST = 1
TILES = 8
SAMPLE_BLOCKS = 2
BAG_BLOCKS = 52
CROSS = 3456
SAMPLES = 8192
ROWS = 16384
N_NODE = 4
N_TABLE = 8
DEVICES = 32


def routing(key):
    stream = jax.random.split(jax.random.fold_in(key, 11), 4)
    groups = N_NODE * N_TABLE
    length = TILE_LIST * N_TABLE
    heavy_count = jax.random.randint(stream[0], (groups, 1), 1, N_TABLE // 4 + 1)
    position = jax.vmap(lambda subkey: jax.random.permutation(subkey, length))(jax.random.split(stream[1], groups))
    shuffle = jax.vmap(lambda subkey: jax.random.permutation(subkey, N_TABLE))(jax.random.split(stream[2], groups))
    heavy_size = 3 * TILE_LIST
    heavy_edge = heavy_size * heavy_count
    leading = position < heavy_edge
    member = jnp.where(leading, position // heavy_size, heavy_count + (position - heavy_edge) // TILE_LIST)
    within = jnp.where(leading, position % heavy_size % (2 * TILE_LIST), (position - heavy_edge) % TILE_LIST)
    table_ids = jnp.take_along_axis(shuffle, member, axis=1)
    base_slot = jax.random.randint(stream[3], (groups, N_TABLE), 0, BAG_BLOCKS)
    slot_ids = (jnp.take_along_axis(base_slot, member, axis=1) + within) % BAG_BLOCKS
    layout = (N_NODE, N_TABLE, N_NODE, length // N_NODE)
    table_out = table_ids.reshape(layout).transpose(2, 1, 0, 3).reshape(-1).astype(jnp.int32)
    slot_out = slot_ids.reshape(layout).transpose(2, 1, 0, 3).reshape(-1).astype(jnp.int32)
    return (table_out, slot_out)


def draw_tile_table(key, part):
    return routing(key)[0]


def draw_tile_slot(key, part):
    return routing(key)[1]


def touch_ends(drawn, own_key, least, top_value):
    longest = drawn.shape.index(max(drawn.shape))
    spots = []
    for shift in (0, 1):
        where = [jax.random.randint(jax.random.fold_in(own_key, axis), (), 0, length) for axis, length in enumerate(drawn.shape)]
        where[longest] = (where[longest] + shift) % drawn.shape[longest]
        spots.append(tuple(where))
    return drawn.at[spots[0]].set(least).at[spots[1]].set(top_value)


def levels(stream_key, extent, cuts, smallest, top_value):
    loudness = 1.0
    for dim, blocks in cuts:
        draws = jax.random.uniform(jax.random.fold_in(jax.random.fold_in(stream_key, 6), dim), (blocks,), jnp.float32, smallest / len(cuts), top_value / len(cuts))
        loudness = loudness * jnp.repeat(jnp.exp(draws), extent[dim] // blocks).reshape((-1,) + (1,) * (len(extent) - 1 - dim))
    return loudness


def centred(rng, shape, spread, limit, cuts=(), held_as=jnp.bfloat16):
    gain = levels(rng, shape, cuts, -0.22, 0.18) if cuts else 1.0
    result = jax.random.normal(rng, shape, jnp.float32) * spread * gain
    return jnp.minimum(jnp.maximum(result, -limit), limit).astype(held_as)


def setup_inputs(seed: int = 0) -> dict:
    arg_keys = jax.random.split(jax.random.key(seed), 11)
    return {
        "emb_rows": centred(arg_keys[0], (ROWS, EMB), 0.04, 0.23925781, ((0, 32),)),
        "tile_mult": touch_ends(jax.random.randint(arg_keys[1], (DEVICES * TILES, BLOCK, BLOCK), 0, 4), jax.random.fold_in(arg_keys[1], 1), 0, 3).astype(jnp.int32),
        "tile_rows": touch_ends(jax.random.randint(arg_keys[2], (DEVICES * TILES,), 0, ROW_BLOCKS), jax.random.fold_in(arg_keys[2], 1), 0, ROW_BLOCKS - 1).astype(jnp.int32),
        "tile_table": draw_tile_table(jax.random.fold_in(arg_keys[10], 71), 0),
        "tile_slot": draw_tile_slot(jax.random.fold_in(arg_keys[10], 71), 0),
        "dense": centred(arg_keys[5], (SAMPLES, EMB), 1.0, 6.0, ((0, 32),)),
        "cross_v": centred(arg_keys[6], (CROSS, RANK), CROSS ** -0.5, 0.109375, ((0, 4),)),
        "cross_u": centred(arg_keys[7], (RANK, CROSS), RANK ** -0.5, 0.25, ((0, 4),)),
        "cross_bias": centred(arg_keys[8], (CROSS,), 0.5, 3.0, (), jnp.float32),
        "cotangent": centred(arg_keys[9], (SAMPLES, CROSS), 0.03, 0.1796875, ((0, 32),)),
    }


def cross_owner(first_layer, cross_v, cross_u, cross_bias, cotangent):
    hidden = jnp.dot(first_layer, cross_v, preferred_element_type=jnp.float32).astype(jnp.bfloat16)
    cross_scale = jnp.dot(hidden, cross_u, preferred_element_type=jnp.float32) + cross_bias
    layer_input = first_layer.astype(jnp.float32)
    cross_out = (layer_input * (cross_scale + 1.0)).astype(jnp.bfloat16)
    upstream = cotangent.astype(jnp.float32)
    dscale = (upstream * layer_input).astype(jnp.bfloat16)
    dhidden = jnp.dot(dscale, cross_u.T, preferred_element_type=jnp.float32).astype(jnp.bfloat16)
    dlayer = upstream * (cross_scale + 1.0) + jnp.dot(dhidden, cross_v.T, preferred_element_type=jnp.float32)
    return cross_out, dlayer[:, EMB:].astype(jnp.bfloat16)


def reference(emb_rows, tile_mult, tile_rows, tile_table, tile_slot, dense, cross_v, cross_u, cross_bias, cotangent):
    devices = N_NODE * N_TABLE
    quarter = TILES // N_NODE
    row_blocks = emb_rows.reshape(devices, ROW_BLOCKS, BLOCK, EMB)
    tile_weights = tile_mult.reshape(devices, TILES, BLOCK, BLOCK)
    dest_node = jnp.arange(TILES, dtype=jnp.int32) // quarter
    owner_ids = dest_node[None, :] * N_TABLE + tile_table.reshape(devices, TILES).astype(jnp.int32)
    bag_index = (owner_ids * BAG_BLOCKS + tile_slot.reshape(devices, TILES).astype(jnp.int32)).astype(jnp.int32)
    rows_local = tile_rows.reshape(devices, TILES).astype(jnp.int32)

    def gather_pool(running, inputs):
        blocks, weights, local_rows, target = inputs
        picked = jnp.take(blocks, local_rows, axis=0).astype(jnp.float32)
        partial_rows = jnp.einsum("kbr,kre->kbe", weights.astype(jnp.float32), picked, precision=lax.Precision.HIGHEST)
        return running.at[target].add(partial_rows), None

    pooled = lax.scan(gather_pool, jnp.zeros((devices * BAG_BLOCKS, BLOCK, EMB), jnp.float32), (row_blocks, tile_weights, rows_local, bag_index))[0]
    embedded = pooled.reshape(devices, FEATURES, SAMPLE_BLOCKS, BLOCK, EMB).transpose(0, 2, 3, 1, 4)
    embedded = embedded.reshape(devices, SAMP_DEV, FEATURES * EMB).astype(jnp.bfloat16)
    first_layer = jnp.concatenate([dense.reshape(devices, SAMP_DEV, EMB), embedded], axis=2)
    cross_out, bag_grad = lax.map(lambda packed: cross_owner(packed[0], cross_v, cross_u, cross_bias, packed[1]), (first_layer, cotangent.reshape(devices, SAMP_DEV, CROSS)))
    bag_grad = bag_grad.reshape(devices, SAMPLE_BLOCKS, BLOCK, FEATURES, EMB).transpose(0, 3, 1, 2, 4)
    bag_grad = bag_grad.reshape(devices * BAG_BLOCKS, BLOCK, EMB)

    def row_grads(inputs):
        weights, local_rows, target = inputs
        back_rows = jnp.take(bag_grad, target, axis=0).astype(jnp.float32)
        tile_grads = jnp.einsum("kbr,kbe->kre", weights.astype(jnp.float32), back_rows, precision=lax.Precision.HIGHEST)
        return jnp.zeros((ROW_BLOCKS, BLOCK, EMB), jnp.float32).at[local_rows].add(tile_grads)

    emb_grad = lax.map(row_grads, (tile_weights, rows_local, bag_index)).reshape(devices * ROW_BLOCKS * BLOCK, EMB)
    return cross_out.reshape(devices * SAMP_DEV, CROSS), emb_grad
```

```python
import functools

import jax
import jax.numpy as jnp
from jax import lax
from jax.experimental import pallas as pl
from jax.experimental.pallas import tpu as pltpu
from jax.sharding import PartitionSpec as P

FEATURES = 26
SAMPLE_BLOCKS = 2
BAG_BLOCKS = 52
LIST = 2
META = 16
BF16 = jnp.bfloat16
F32 = jnp.float32
SMEM = pl.BlockSpec(memory_space=pltpu.SMEM)
VMEM = pl.BlockSpec(memory_space=pltpu.VMEM)


def params(mib):
    return pltpu.CompilerParams(vmem_limit_bytes=mib << 20)


def nt_dot(left, right):
    return lax.dot_general(left, right, (((1,), (1,)), ((), ())), preferred_element_type=F32)


def tn_dot(left, right):
    return lax.dot_general(left, right, (((0,), (0,)), ((), ())), preferred_element_type=F32)


def dot(left, right):
    return jnp.dot(left, right, preferred_element_type=F32)


def block(index, size):
    return pl.ds(pl.multiple_of(index * size, size), size)


def meta_rows(count):
    return -(-2 * count // 16) * 16


def id_rows(values, rows):
    row = lax.broadcasted_iota(jnp.int32, (rows, 128), 0)
    filled = jnp.full((rows, 128), -1.0, F32)
    for i, value in enumerate(values):
        filled = jnp.where(row == i, value.astype(F32), filled)
    return filled.astype(BF16)


def products_kernel(nodes, quota, size, place_ref, rows_ref, table_ref, slot_ref, emb_ref, mult_ref, *outs):
    node = place_ref[0]
    for k in range(nodes):
        ids = []
        for i in range(quota):
            tile = (node ^ k) * quota + i
            weights = mult_ref[tile].astype(F32).astype(BF16)
            part = dot(weights, emb_ref[block(rows_ref[tile], size), :])
            outs[k][i * size : (i + 1) * size, :] = part.astype(BF16)
            ids += [table_ref[tile], slot_ref[tile]]
        outs[k][quota * size :, :] = id_rows(ids, meta_rows(quota))


def relay_kernel(nodes, quota, size, tables, relative, place_ref, *refs):
    parts, outs = refs[:nodes], refs[nodes : nodes + tables]
    index_ref, total, first_slot, slots = refs[nodes + tables :]
    table = place_ref[1]
    for r in range(tables):
        first_slot[r] = -1
        for e in range(LIST):
            slots[r * LIST + e] = -1
            total[r * LIST + e] = jnp.zeros((size, 128), F32)
    for k in range(nodes):
        ids = parts[k][quota * size :, :].astype(F32).astype(jnp.int32)
        for i in range(quota):
            target, slot = ids[2 * i, 0], ids[2 * i + 1, 0]
            entry = target ^ table if relative else target
            known = first_slot[entry]
            which = jnp.where((known < 0) | (known == slot), 0, 1)
            first_slot[entry] = jnp.where(known < 0, slot, known)
            place = entry * LIST + which
            slots[place] = slot
            index_ref[k * quota + i] = place
            total[place] += parts[k][i * size : (i + 1) * size, :].astype(F32)
    for r in range(tables):
        for e in range(LIST):
            outs[r][e * size : (e + 1) * size, :] = total[r * LIST + e].astype(BF16)
        outs[r][LIST * size :, :] = id_rows([slots[r * LIST + e] for e in range(LIST)], META)


def owner_kernel(tables, size, *refs):
    parts = refs[:tables]
    dense_ref, v_ref, u_ref, bias_ref, cot_ref = refs[tables : tables + 5]
    outs = refs[tables + 5 : 2 * tables + 5]
    first_ref, hidden_ref, total, scaled, dhidden = refs[2 * tables + 5 :]
    for b in range(BAG_BLOCKS):
        total[b] = jnp.zeros((size, 128), F32)
    slots = []
    for r in range(tables):
        ids = parts[r][LIST * size :, :].astype(F32).astype(jnp.int32)
        for e in range(LIST):
            slots.append(ids[e, 0])

            @pl.when(slots[-1] >= 0)
            def _(slot=slots[-1], r=r, e=e):
                total[slot] += parts[r][e * size : (e + 1) * size, :].astype(F32)

    first_ref[:, :128] = dense_ref[...]
    for f in range(FEATURES):
        for s in range(SAMPLE_BLOCKS):
            first_ref[s * size : (s + 1) * size, (f + 1) * 128 : (f + 2) * 128] = total[f * SAMPLE_BLOCKS + s].astype(BF16)
    hidden_ref[...] = dot(first_ref[...], v_ref[...]).astype(BF16)
    for f in range(FEATURES + 1):
        columns = slice(f * 128, (f + 1) * 128)
        scaled[:, columns] = (cot_ref[:, columns].astype(F32) * first_ref[:, columns].astype(F32)).astype(BF16)
    dhidden[...] = nt_dot(scaled[...], u_ref[...]).astype(BF16)
    for r in range(tables):
        for e in range(LIST):

            @pl.when(slots[r * LIST + e] >= 0)
            def _(slot=slots[r * LIST + e], r=r, e=e):
                columns = block(slot // SAMPLE_BLOCKS + 1, 128)
                samples = block(slot % SAMPLE_BLOCKS, size)
                scale = dot(hidden_ref[samples, :], u_ref[:, columns]) + bias_ref[:, columns]
                grad = cot_ref[samples, columns].astype(F32) * (scale + 1.0)
                grad = grad + nt_dot(dhidden[samples, :], v_ref[columns, :])
                outs[r][e * size : (e + 1) * size, :] = grad.astype(BF16)


def cross_kernel(first_ref, hidden_ref, u_ref, bias_ref, out_ref):
    width = first_ref.shape[1]
    step = 256
    for start in range(0, width, step):
        columns = slice(start, min(start + step, width))
        scale = dot(hidden_ref[...], u_ref[:, columns]) + bias_ref[:, columns]
        out_ref[:, columns] = (first_ref[:, columns].astype(F32) * (scale + 1.0)).astype(BF16)


def return_kernel(nodes, quota, size, tables, index_ref, *refs):
    parts, outs, staged = refs[:tables], refs[tables : tables + nodes], refs[-1]
    for r in range(tables):
        for e in range(LIST):
            staged[r * LIST + e] = parts[r][e * size : (e + 1) * size, :]
    for k in range(nodes):
        for i in range(quota):
            outs[k][i * size : (i + 1) * size, :] = staged[index_ref[k * quota + i]]


def rows_kernel(nodes, quota, size, place_ref, rows_ref, mult_ref, *refs):
    parts, out_ref = refs[:nodes], refs[nodes]
    node = place_ref[0]
    out_ref[...] = jnp.zeros(out_ref.shape, F32)
    for k in range(nodes):
        for i in range(quota):
            tile = (node ^ k) * quota + i
            weights = mult_ref[tile].astype(F32).astype(BF16)
            rows = block(rows_ref[tile], size)
            out_ref[rows, :] += tn_dot(weights, parts[k][i * size : (i + 1) * size, :])


def xor_permute(value, axis, k):
    size = lax.axis_size(axis)
    return lax.ppermute(value, axis, [(i, i ^ k) for i in range(size)])


def exchange_tables(parts):
    tables = len(parts)
    out = [None] * tables
    out[0] = parts[0]
    order = sorted(range(2, tables), key=lambda r: (-(r // 4), r))
    for r in order:
        out[r] = xor_permute(parts[r], "table", r)
    out[1] = xor_permute(parts[1], "table", 1)
    return out


def exchange_tables_whole(parts):
    moved = lax.all_to_all(jnp.stack(parts), "table", split_axis=0, concat_axis=0, tiled=True)
    return [moved[r] for r in range(len(parts))]


def gather_weights(cross_v, cross_u):
    node = lax.axis_index("node")
    core = lax.axis_index("table") % 2

    def gathered(shard):
        rows, width = shard.shape
        half = rows // 2
        cut = half // 32 * 16
        mine = lax.dynamic_slice(shard, (core * half, 0), (half, width))
        by_x = xor_permute(mine, "node", 1)
        by_y = xor_permute(mine, "node", 2)
        far_x = xor_permute(by_y[:cut], "node", 1)
        far_y = xor_permute(by_x[cut:], "node", 2)
        whole = jnp.zeros((rows * lax.axis_size("node"), width), shard.dtype)
        whole = lax.dynamic_update_slice(whole, shard, (node * rows, 0))
        for k, begin, piece in ((1, 0, by_x), (2, 0, by_y), (3, 0, far_x), (3, cut, far_y)):
            base = (node ^ k) * rows + begin
            whole = lax.dynamic_update_slice(whole, piece, (base + core * half, 0))
            other = xor_permute(piece, "table", 1)
            whole = lax.dynamic_update_slice(whole, other, (base + (1 - core) * half, 0))
        return whole

    return gathered(cross_v), gathered(cross_u)


def body(emb_rows, tile_mult, tile_rows, tile_table, tile_slot, dense, cross_v, cross_u, cross_bias, cotangent):
    nodes, tables = lax.axis_size("node"), lax.axis_size("table")
    tiles, size = tile_mult.shape[0], tile_mult.shape[1]
    quota = tiles // nodes
    samples, cross = cotangent.shape
    rank = cross_v.shape[1]
    relative = tables <= 8
    exchange = exchange_tables if relative else exchange_tables_whole
    place = jnp.stack([lax.axis_index("node"), lax.axis_index("table")]).astype(jnp.int32)
    bias = cross_bias.reshape(1, cross)

    full_v, full_u = gather_weights(cross_v, cross_u)

    part = jax.ShapeDtypeStruct((quota * size + meta_rows(quota), 128), BF16)
    parts = pl.pallas_call(
        functools.partial(products_kernel, nodes, quota, size),
        out_shape=[part] * nodes,
        in_specs=[SMEM] * 4 + [VMEM] * 2,
        out_specs=[VMEM] * nodes,
        compiler_params=params(16),
        name="products",
    )(place, tile_rows, tile_table, tile_slot, emb_rows, tile_mult)
    parts = [parts[0]] + [xor_permute(parts[k], "node", k) for k in range(1, nodes)]

    listed = jax.ShapeDtypeStruct((LIST * size + META, 128), BF16)
    *lists, index = pl.pallas_call(
        functools.partial(relay_kernel, nodes, quota, size, tables, relative),
        out_shape=[listed] * tables + [jax.ShapeDtypeStruct((tiles,), jnp.int32)],
        in_specs=[SMEM] + [VMEM] * nodes,
        out_specs=[VMEM] * tables + [SMEM],
        scratch_shapes=[
            pltpu.VMEM((tables * LIST, size, 128), F32),
            pltpu.SMEM((tables,), jnp.int32),
            pltpu.SMEM((tables * LIST,), jnp.int32),
        ],
        compiler_params=params(32),
        name="relay",
    )(place, *parts)
    arrived = exchange(lists)

    grad = jax.ShapeDtypeStruct((LIST * size, 128), BF16)
    *grads, first, hidden = pl.pallas_call(
        functools.partial(owner_kernel, tables, size),
        out_shape=[grad] * tables
        + [jax.ShapeDtypeStruct((samples, cross), BF16), jax.ShapeDtypeStruct((samples, rank), BF16)],
        in_specs=[VMEM] * (tables + 5),
        out_specs=[VMEM] * (tables + 2),
        scratch_shapes=[
            pltpu.VMEM((BAG_BLOCKS, size, 128), F32),
            pltpu.VMEM((samples, cross), BF16),
            pltpu.VMEM((samples, rank), BF16),
        ],
        compiler_params=params(48),
        name="owner",
    )(*arrived, dense, full_v, full_u, bias, cotangent)
    returned = exchange(grads)

    cross_out = pl.pallas_call(
        cross_kernel,
        out_shape=jax.ShapeDtypeStruct((samples, cross), BF16),
        in_specs=[VMEM] * 4,
        out_specs=VMEM,
        compiler_params=params(32),
        name="cross",
    )(first, hidden, full_u, bias)

    back = jax.ShapeDtypeStruct((quota * size, 128), BF16)
    backs = pl.pallas_call(
        functools.partial(return_kernel, nodes, quota, size, tables),
        out_shape=[back] * nodes,
        in_specs=[SMEM] + [VMEM] * tables,
        out_specs=[VMEM] * nodes,
        scratch_shapes=[pltpu.VMEM((tables * LIST, size, 128), BF16)],
        compiler_params=params(32),
        name="back",
    )(index, *returned)
    backs = [backs[0]] + [xor_permute(backs[k], "node", k) for k in range(1, nodes)]

    emb_grad = pl.pallas_call(
        functools.partial(rows_kernel, nodes, quota, size),
        out_shape=jax.ShapeDtypeStruct(emb_rows.shape, F32),
        in_specs=[SMEM] * 2 + [VMEM] * (nodes + 1),
        out_specs=VMEM,
        compiler_params=params(16),
        name="rows",
    )(place, tile_rows, tile_mult, *backs)
    return cross_out, emb_grad


def solution(mesh):
    both = ("node", "table")
    in_specs = (
        P(both, None),
        P(both, None, None),
        P(both),
        P(both),
        P(both),
        P(both, None),
        P("node", None),
        P("node", None),
        P(),
        P(both, None),
    )
    out_specs = (P(both, None), P(both, None))
    return jax.shard_map(body, mesh=mesh, in_specs=in_specs, out_specs=out_specs, check_vma=False)
```

```python
import functools

import jax
import jax.numpy as jnp
from jax import lax
from jax.experimental import pallas as pl
from jax.experimental.pallas import tpu as pltpu
from jax.sharding import PartitionSpec as P

FEATURES = 26
SAMPLE_BLOCKS = 2
BAG_BLOCKS = 52
CORES = 2
LIST = 2
META = 16
FIRST = 5 * 10**10
BF16 = jnp.bfloat16
F32 = jnp.float32
SMEM = pl.BlockSpec(memory_space=pltpu.SMEM)
VMEM = pl.BlockSpec(memory_space=pltpu.VMEM)


def params(mib):
    return pltpu.CompilerParams(vmem_limit_bytes=mib << 20)


def nt_dot(left, right):
    return lax.dot_general(left, right, (((1,), (1,)), ((), ())), preferred_element_type=F32)


def tn_dot(left, right):
    return lax.dot_general(left, right, (((0,), (0,)), ((), ())), preferred_element_type=F32)


def dot(left, right):
    return jnp.dot(left, right, preferred_element_type=F32)


def block(index, size):
    return pl.ds(pl.multiple_of(index * size, size), size)


def meta_rows(count):
    return -(-2 * count // 16) * 16


def id_rows(values, rows):
    row = lax.broadcasted_iota(jnp.int32, (rows, 128), 0)
    filled = jnp.full((rows, 128), -1.0, F32)
    for i, value in enumerate(values):
        filled = jnp.where(row == i, value.astype(F32), filled)
    return filled.astype(BF16)


def products_kernel(nodes, quota, size, rows_hbm, table_hbm, slot_hbm, emb_hbm, mult_hbm, *refs):
    outs = refs[:nodes]
    rows_ref, table_ref, slot_ref, emb_ref, mult_ref, sems = refs[nodes:]
    pairs = ((mult_hbm, mult_ref), (emb_hbm, emb_ref), (rows_hbm, rows_ref), (table_hbm, table_ref), (slot_hbm, slot_ref))
    copies = [pltpu.make_async_copy(src, dst, sems.at[i]) for i, (src, dst) in enumerate(pairs)]
    for copy in copies:
        copy.start()
    for copy in copies:
        copy.wait()
    node = lax.axis_index("node")
    for k in range(nodes):
        ids = []
        for i in range(quota):
            tile = (node ^ k) * quota + i
            weights = mult_ref[tile].astype(F32).astype(BF16)
            part = dot(weights, emb_ref[block(rows_ref[tile], size), :])
            outs[k][i * size : (i + 1) * size, :] = part.astype(BF16)
            ids += [table_ref[tile], slot_ref[tile]]
        outs[k][quota * size :, :] = id_rows(ids, meta_rows(quota))


def relay_kernel(nodes, quota, size, tables, relative, *refs):
    chips = tables // CORES
    parts, outs = refs[:nodes], refs[nodes : nodes + chips]
    index_ref, total, first_slot, slots = refs[nodes + chips :]
    table = lax.axis_index("table")
    for r in range(tables):
        first_slot[r] = -1
        for e in range(LIST):
            slots[r * LIST + e] = -1
            total[r * LIST + e] = jnp.zeros((size, 128), F32)
    for k in range(nodes):
        ids = parts[k][quota * size :, :].astype(F32).astype(jnp.int32)
        for i in range(quota):
            target, slot = ids[2 * i, 0], ids[2 * i + 1, 0]
            entry = target ^ table if relative else target
            known = first_slot[entry]
            which = jnp.where((known < 0) | (known == slot), 0, 1)
            first_slot[entry] = jnp.where(known < 0, slot, known)
            place = entry * LIST + which
            slots[place] = slot
            index_ref[k * quota + i] = place
            total[place] += parts[k][i * size : (i + 1) * size, :].astype(F32)
    for r in range(tables):
        out, base = outs[r // CORES], r % CORES * (LIST * size + META)
        for e in range(LIST):
            out[base + e * size : base + (e + 1) * size, :] = total[r * LIST + e].astype(BF16)
        base += LIST * size
        out[base : base + META, :] = id_rows([slots[r * LIST + e] for e in range(LIST)], META)


def pool_kernel(tables, size, *refs):
    parts = refs[:tables]
    dense_ref, v_ref, cot_ref, first_ref, hidden_ref, scaled_ref, slot_ref, total = refs[tables:]
    for b in range(BAG_BLOCKS):
        total[b] = jnp.zeros((size, 128), F32)
    for r in range(tables):
        part, base = parts[r], r % CORES * (LIST * size + META)
        ids = part[base + LIST * size : base + LIST * size + META, :].astype(F32).astype(jnp.int32)
        for e in range(LIST):
            slot_ref[r * LIST + e] = ids[e, 0]

            @pl.when(ids[e, 0] >= 0)
            def _(slot=ids[e, 0], part=part, begin=base + e * size):
                total[slot] += part[begin : begin + size, :].astype(F32)

    first_ref[:, :128] = dense_ref[...]
    for f in range(FEATURES):
        for s in range(SAMPLE_BLOCKS):
            columns = slice((f + 1) * 128, (f + 2) * 128)
            first_ref[s * size : (s + 1) * size, columns] = total[f * SAMPLE_BLOCKS + s].astype(BF16)
    hidden_ref[...] = dot(first_ref[...], v_ref[...]).astype(BF16)
    for f in range(FEATURES + 1):
        columns = slice(f * 128, (f + 1) * 128)
        scaled_ref[:, columns] = (cot_ref[:, columns].astype(F32) * first_ref[:, columns].astype(F32)).astype(BF16)


def owner_kernel(tables, size, slot_ref, hidden_ref, scaled_ref, v_ref, u_ref, bias_ref, cot_ref, *refs):
    outs, dhidden = refs[: tables // CORES], refs[tables // CORES]
    dhidden[...] = nt_dot(scaled_ref[...], u_ref[...]).astype(BF16)
    for r in range(tables):
        for e in range(LIST):
            slot = slot_ref[r * LIST + e]

            @pl.when(slot >= 0)
            def _(slot=slot, out=outs[r // CORES], begin=(r % CORES * LIST + e) * size):
                columns = block(slot // SAMPLE_BLOCKS + 1, 128)
                samples = block(slot % SAMPLE_BLOCKS, size)
                scale = dot(hidden_ref[samples, :], u_ref[:, columns]) + bias_ref[:, columns]
                grad = cot_ref[samples, columns].astype(F32) * (scale + 1.0)
                grad = grad + nt_dot(dhidden[samples, :], v_ref[columns, :])
                out[begin : begin + size, :] = grad.astype(BF16)


def cross_kernel(first_ref, hidden_ref, u_ref, bias_ref, out_ref):
    width = first_ref.shape[1]
    step = 256
    for start in range(0, width, step):
        columns = slice(start, min(start + step, width))
        scale = dot(hidden_ref[...], u_ref[:, columns]) + bias_ref[:, columns]
        out_ref[:, columns] = (first_ref[:, columns].astype(F32) * (scale + 1.0)).astype(BF16)


def return_kernel(nodes, quota, size, tables, index_ref, *refs):
    parts, outs, staged = refs[:tables], refs[tables : tables + nodes], refs[-1]
    for r in range(tables):
        for e in range(LIST):
            begin = (r % CORES * LIST + e) * size
            staged[r * LIST + e] = parts[r][begin : begin + size, :]
    for k in range(nodes):
        for i in range(quota):
            outs[k][i * size : (i + 1) * size, :] = staged[index_ref[k * quota + i]]


def rows_kernel(nodes, quota, size, rows_ref, mult_ref, *refs):
    parts, out_ref = refs[:nodes], refs[nodes]
    node = lax.axis_index("node")
    out_ref[...] = jnp.zeros(out_ref.shape, F32)
    for k in range(nodes):
        for i in range(quota):
            tile = (node ^ k) * quota + i
            weights = mult_ref[tile].astype(F32).astype(BF16)
            rows = block(rows_ref[tile], size)
            out_ref[rows, :] += tn_dot(weights, parts[k][i * size : (i + 1) * size, :])


def xor_permute(value, axis, k):
    size = lax.axis_size(axis)
    return lax.ppermute(value, axis, [(i, i ^ k) for i in range(size)])


def exchange_chips(parts):
    return [parts[0]] + [xor_permute(parts[k], "table", CORES * k) for k in range(1, len(parts))]


def exchange_cores(parts):
    return [item for part in parts for item in (part, sibling(part))]


def exchange_whole(parts):
    height = parts[0].shape[0] // CORES
    stacked = jnp.stack(parts).reshape(len(parts) * CORES, height, parts[0].shape[1])
    moved = lax.all_to_all(stacked, "table", split_axis=0, concat_axis=0, tiled=True)
    moved = moved.reshape(len(parts), CORES * height, parts[0].shape[1])
    return [moved[r // CORES] for r in range(len(parts) * CORES)]


def permute(value, target):
    nodes, tables = lax.axis_size("node"), lax.axis_size("table")
    pairs = []
    for n in range(nodes):
        for t in range(tables):
            m, s = target(n, t)
            pairs.append((n * tables + t, m * tables + s))
    return lax.ppermute(value, ("node", "table"), pairs)


def near(value):
    return permute(value, lambda n, t: (n ^ (1 + t % 2), t))


def far(value):
    return permute(value, lambda n, t: (n ^ (2 - t % 2), t))


def sibling(value):
    return permute(value, lambda n, t: (n, t ^ 1))


def half_of(shard):
    half = shard.shape[0] // 2
    core = lax.axis_index("table") % 2
    return lax.dynamic_slice(shard, (core * half, 0), (half, shard.shape[1]))


def assemble(shard, first, first_other, second, second_other):
    node = lax.axis_index("node")
    core = lax.axis_index("table") % 2
    rows, width = shard.shape
    half = rows // 2
    whole = jnp.zeros((rows * lax.axis_size("node"), width), shard.dtype)
    for piece, row in (
        (shard, node * rows),
        (first, (node ^ (1 + core)) * rows),
        (first_other, (node ^ (2 - core)) * rows),
        (second, (node ^ 3) * rows + core * half),
        (second_other, (node ^ 3) * rows + (1 - core) * half),
    ):
        whole = lax.dynamic_update_slice(whole, piece, (row, 0))
    return whole


def body(emb_rows, tile_mult, tile_rows, tile_table, tile_slot, dense, cross_v, cross_u, cross_bias, cotangent):
    nodes, tables = lax.axis_size("node"), lax.axis_size("table")
    tiles, size = tile_mult.shape[0], tile_mult.shape[1]
    quota = tiles // nodes
    samples, cross = cotangent.shape
    rank = cross_v.shape[1]
    relative = tables <= 8
    bias = cross_bias.reshape(1, cross)

    part = jax.ShapeDtypeStruct((quota * size + meta_rows(quota), 128), BF16)
    hbm = pl.BlockSpec(memory_space=pltpu.HBM)
    parts = pl.pallas_call(
        functools.partial(products_kernel, nodes, quota, size),
        out_shape=[part] * nodes,
        in_specs=[hbm] * 5,
        out_specs=[VMEM] * nodes,
        scratch_shapes=[
            pltpu.SMEM((tiles,), jnp.int32),
            pltpu.SMEM((tiles,), jnp.int32),
            pltpu.SMEM((tiles,), jnp.int32),
            pltpu.VMEM(emb_rows.shape, BF16),
            pltpu.VMEM(tile_mult.shape, jnp.int32),
            pltpu.SemaphoreType.DMA((5,)),
        ],
        compiler_params=params(60),
        name="products",
    )(tile_rows, tile_table, tile_slot, emb_rows, tile_mult)
    first_v = near(cross_v)
    parts = [parts[0]] + [xor_permute(parts[k], "node", k) for k in range(1, nodes)]
    late_u, parts[1] = lax.optimization_barrier((cross_u, parts[1]))
    first_u = near(late_u)
    second_v = far(half_of(first_v))
    second_u = far(half_of(first_u))

    chips = tables // CORES
    listed = jax.ShapeDtypeStruct((CORES * (LIST * size + META), 128), BF16)
    *lists, index = pl.pallas_call(
        functools.partial(relay_kernel, nodes, quota, size, tables, relative),
        out_shape=[listed] * chips + [jax.ShapeDtypeStruct((tiles,), jnp.int32)],
        in_specs=[VMEM] * nodes,
        out_specs=[VMEM] * chips + [SMEM],
        scratch_shapes=[
            pltpu.VMEM((tables * LIST, size, 128), F32),
            pltpu.SMEM((tables,), jnp.int32),
            pltpu.SMEM((tables * LIST,), jnp.int32),
        ],
        compiler_params=params(32),
        cost_estimate=pl.CostEstimate(flops=FIRST, bytes_accessed=0, transcendentals=0),
        name="relay",
    )(*parts)
    if relative:
        first_v, second_v, *arrived = lax.optimization_barrier((first_v, second_v, *exchange_chips(lists)))
        arrived = exchange_cores(arrived)
    else:
        arrived = exchange_whole(lists)
    full_v = assemble(cross_v, first_v, sibling(first_v), second_v, sibling(second_v))

    grad = jax.ShapeDtypeStruct((CORES * LIST * size, 128), BF16)
    first, hidden, scaled, slots = pl.pallas_call(
        functools.partial(pool_kernel, tables, size),
        out_shape=[
            jax.ShapeDtypeStruct((samples, cross), BF16),
            jax.ShapeDtypeStruct((samples, rank), BF16),
            jax.ShapeDtypeStruct((samples, cross), BF16),
            jax.ShapeDtypeStruct((tables * LIST,), jnp.int32),
        ],
        in_specs=[VMEM] * (tables + 3),
        out_specs=[VMEM] * 3 + [SMEM],
        scratch_shapes=[pltpu.VMEM((BAG_BLOCKS, size, 128), F32)],
        compiler_params=params(24),
        name="pool",
    )(*arrived, dense, full_v, cotangent)

    if relative:
        second_u, hidden = lax.optimization_barrier((second_u, hidden))
    full_u = assemble(cross_u, first_u, sibling(first_u), second_u, sibling(second_u))

    grads = pl.pallas_call(
        functools.partial(owner_kernel, tables, size),
        out_shape=[grad] * chips,
        in_specs=[SMEM] + [VMEM] * 6,
        out_specs=[VMEM] * chips,
        scratch_shapes=[pltpu.VMEM((samples, rank), BF16)],
        compiler_params=params(24),
        name="owner",
    )(slots, hidden, scaled, full_v, full_u, bias, cotangent)
    cross_out = pl.pallas_call(
        cross_kernel,
        out_shape=jax.ShapeDtypeStruct((samples, cross), BF16),
        in_specs=[VMEM] * 4,
        out_specs=VMEM,
        compiler_params=params(32),
        cost_estimate=pl.CostEstimate(
            flops=2 * samples * rank * cross, bytes_accessed=4 * samples * cross + 2 * rank * cross, transcendentals=0
        ),
        name="cross",
    )(first, hidden, full_u, bias)

    if relative:
        returned = exchange_chips(grads)
        returned[-1], cross_out = lax.optimization_barrier((returned[-1], cross_out))
        returned = exchange_cores(returned)
    else:
        returned = exchange_whole(grads)

    back = jax.ShapeDtypeStruct((quota * size, 128), BF16)
    backs = pl.pallas_call(
        functools.partial(return_kernel, nodes, quota, size, tables),
        out_shape=[back] * nodes,
        in_specs=[SMEM] + [VMEM] * tables,
        out_specs=[VMEM] * nodes,
        scratch_shapes=[pltpu.VMEM((tables * LIST, size, 128), BF16)],
        compiler_params=params(32),
        name="back",
    )(index, *returned)
    backs = [backs[0]] + [xor_permute(backs[k], "node", k) for k in range(1, nodes)]

    emb_grad = pl.pallas_call(
        functools.partial(rows_kernel, nodes, quota, size),
        out_shape=jax.ShapeDtypeStruct(emb_rows.shape, F32),
        in_specs=[SMEM] + [VMEM] * (nodes + 1),
        out_specs=VMEM,
        compiler_params=params(16),
        name="rows",
    )(tile_rows, tile_mult, *backs)
    return cross_out, emb_grad


def solution(mesh):
    both = ("node", "table")
    in_specs = (
        P(both, None),
        P(both, None, None),
        P(both),
        P(both),
        P(both),
        P(both, None),
        P("node", None),
        P("node", None),
        P(),
        P(both, None),
    )
    out_specs = (P(both, None), P(both, None))
    return jax.shard_map(body, mesh=mesh, in_specs=in_specs, out_specs=out_specs, check_vma=False)
```

```python
import functools

import jax
import jax.numpy as jnp
from jax import lax
from jax.experimental import pallas as pl
from jax.experimental.pallas import tpu as pltpu
from jax.sharding import PartitionSpec as P

FEATURES = 26
SAMPLE_BLOCKS = 2
BAG_BLOCKS = 52
CORES = 2
LIST = 2
META = 16
RELAY_FLOPS = 10**6
BF16 = jnp.bfloat16
F32 = jnp.float32
SMEM = pl.BlockSpec(memory_space=pltpu.SMEM)
VMEM = pl.BlockSpec(memory_space=pltpu.VMEM)


def params(mib):
    return pltpu.CompilerParams(vmem_limit_bytes=mib << 20)


def nt_dot(left, right):
    return lax.dot_general(left, right, (((1,), (1,)), ((), ())), preferred_element_type=F32)


def tn_dot(left, right):
    return lax.dot_general(left, right, (((0,), (0,)), ((), ())), preferred_element_type=F32)


def dot(left, right):
    return jnp.dot(left, right, preferred_element_type=F32)


def block(index, size):
    return pl.ds(pl.multiple_of(index * size, size), size)


def meta_rows(count):
    return -(-2 * count // 16) * 16


def id_rows(values, rows):
    row = lax.broadcasted_iota(jnp.int32, (rows, 128), 0)
    filled = jnp.full((rows, 128), -1.0, F32)
    for i, value in enumerate(values):
        filled = jnp.where(row == i, value.astype(F32), filled)
    return filled.astype(BF16)


def swap_bits(core):
    return 1 + core, 2 - core


def products_kernel(quota, size, rows_hbm, table_hbm, slot_hbm, emb_hbm, mult_hbm, *refs):
    outs = refs[:5]
    rows_ref, table_ref, slot_ref, emb_ref, mult_ref, sems = refs[5:]
    pairs = ((mult_hbm, mult_ref), (emb_hbm, emb_ref), (rows_hbm, rows_ref), (table_hbm, table_ref), (slot_hbm, slot_ref))
    copies = [pltpu.make_async_copy(src, dst, sems.at[i]) for i, (src, dst) in enumerate(pairs)]
    for copy in copies:
        copy.start()
    for copy in copies:
        copy.wait()
    node = lax.axis_index("node")
    near_bit, far_bit = swap_bits(lax.axis_index("table") % CORES)
    own, far_out, opposite, hop_near, hop_opposite = outs
    for out, k in ((far_out, far_bit), (hop_near, near_bit), (opposite, 3), (own, 0)):
        ids = []
        for i in range(quota):
            tile = (node ^ k) * quota + i
            weights = mult_ref[tile].astype(F32).astype(BF16)
            part = dot(weights, emb_ref[block(rows_ref[tile], size), :])
            out[i * size : (i + 1) * size, :] = part.astype(BF16)
            ids += [table_ref[tile], slot_ref[tile]]
        out[quota * size :, :] = id_rows(ids, meta_rows(quota))
    hop_opposite[...] = opposite[...]


def relay_kernel(quota, size, tables, relative, *refs):
    chips = tables // CORES
    own, by_far, by_near, opposite, opposite_hop = refs[:5]
    outs = refs[5 : 5 + chips]
    index_ref, total, first_slot, slots = refs[5 + chips :]
    table = lax.axis_index("table")
    for r in range(tables):
        first_slot[r] = -1
        for e in range(LIST):
            slots[r * LIST + e] = -1
            total[r * LIST + e] = jnp.zeros((size, 128), F32)
    core = table % CORES
    near_bit, far_bit = swap_bits(core)

    def rows_of(part, rows):
        if part is opposite:
            return jnp.where(core == 1, opposite[rows, :].astype(F32), opposite_hop[rows, :].astype(F32))
        return part[rows, :].astype(F32)

    for part, k in ((own, 0), (by_far, far_bit), (by_near, near_bit), (opposite, 3)):
        ids = rows_of(part, slice(quota * size, None)).astype(jnp.int32)
        for i in range(quota):
            target, slot = ids[2 * i, 0], ids[2 * i + 1, 0]
            entry = target ^ table if relative else target
            known = first_slot[entry]
            which = jnp.where((known < 0) | (known == slot), 0, 1)
            first_slot[entry] = jnp.where(known < 0, slot, known)
            place = entry * LIST + which
            slots[place] = slot
            index_ref[k * quota + i] = place
            total[place] += rows_of(part, slice(i * size, (i + 1) * size))
    for r in range(tables):
        out, base = outs[r // CORES], r % CORES * (LIST * size + META)
        for e in range(LIST):
            out[base + e * size : base + (e + 1) * size, :] = total[r * LIST + e].astype(BF16)
        base += LIST * size
        out[base : base + META, :] = id_rows([slots[r * LIST + e] for e in range(LIST)], META)


def pool_kernel(tables, size, *refs):
    parts = refs[:tables]
    dense_ref, cot_ref, v_ref, first_ref, scaled_ref, slot_ref, hidden_ref, total = refs[tables:]
    for b in range(BAG_BLOCKS + 1):
        total[b] = jnp.zeros((size, 128), F32)
    for r in range(tables):
        part, base = parts[r], r % CORES * (LIST * size + META)
        ids = part[base + LIST * size : base + LIST * size + META, :].astype(F32).astype(jnp.int32)
        for e in range(LIST):
            slot_ref[r * LIST + e] = ids[e, 0]
            begin = base + e * size
            place = jnp.where(ids[e, 0] < 0, BAG_BLOCKS, ids[e, 0])
            total[place] += part[begin : begin + size, :].astype(F32)

    first_ref[:, :128] = dense_ref[...]
    for f in range(FEATURES):
        for s in range(SAMPLE_BLOCKS):
            columns = slice((f + 1) * 128, (f + 2) * 128)
            first_ref[s * size : (s + 1) * size, columns] = total[f * SAMPLE_BLOCKS + s].astype(BF16)
    hidden_ref[...] = dot(first_ref[...], v_ref[...]).astype(BF16)
    for f in range(FEATURES + 1):
        columns = slice(f * 128, (f + 1) * 128)
        scaled_ref[:, columns] = (cot_ref[:, columns].astype(F32) * first_ref[:, columns].astype(F32)).astype(BF16)


def blocks_kernel(group, size, slot_ref, hidden_ref, dhidden_ref, v_ref, u_ref, bias_ref, cot_ref, *outs):
    for chip, out in zip(group, outs):
        for entry in range(CORES * LIST):
            slot = jnp.maximum(slot_ref[chip * CORES * LIST + entry], 0)
            columns = block(slot // SAMPLE_BLOCKS + 1, 128)
            samples = block(slot % SAMPLE_BLOCKS, size)
            scale = dot(hidden_ref[samples, :], u_ref[:, columns]) + bias_ref[:, columns]
            grad = cot_ref[samples, columns].astype(F32) * (scale + 1.0)
            grad = grad + nt_dot(dhidden_ref[samples, :], v_ref[columns, :])
            out[entry * size : (entry + 1) * size, :] = grad.astype(BF16)


def owner_kernel(group, size, slot_ref, hidden_ref, scaled_ref, v_ref, u_ref, bias_ref, cot_ref, *outs):
    dhidden_ref = outs[-1]
    dhidden_ref[...] = nt_dot(scaled_ref[...], u_ref[...]).astype(BF16)
    blocks_kernel(group, size, slot_ref, hidden_ref, dhidden_ref, v_ref, u_ref, bias_ref, cot_ref, *outs[:-1])


def cross_kernel(first_ref, hidden_ref, u_ref, bias_ref, out_ref):
    width = first_ref.shape[1]
    step = 256
    for start in range(0, width, step):
        columns = slice(start, min(start + step, width))
        scale = dot(hidden_ref[...], u_ref[:, columns]) + bias_ref[:, columns]
        out_ref[:, columns] = (first_ref[:, columns].astype(F32) * (scale + 1.0)).astype(BF16)


def return_kernel(nodes, quota, size, tables, index_ref, *refs):
    parts, outs, staged = refs[:tables], refs[tables : tables + nodes], refs[-1]
    for r in range(tables):
        for e in range(LIST):
            begin = (r % CORES * LIST + e) * size
            staged[r * LIST + e] = parts[r][begin : begin + size, :]
    for k in range(nodes):
        for i in range(quota):
            outs[k][i * size : (i + 1) * size, :] = staged[index_ref[k * quota + i]]


def rows_kernel(nodes, quota, size, rows_ref, mult_ref, *refs):
    parts, out_ref = refs[:nodes], refs[nodes]
    node = lax.axis_index("node")
    out_ref[...] = jnp.zeros(out_ref.shape, F32)
    for k in range(nodes):
        for i in range(quota):
            tile = (node ^ k) * quota + i
            weights = mult_ref[tile].astype(F32).astype(BF16)
            rows = block(rows_ref[tile], size)
            out_ref[rows, :] += tn_dot(weights, parts[k][i * size : (i + 1) * size, :])


def xor_permute(value, axis, k):
    size = lax.axis_size(axis)
    return lax.ppermute(value, axis, [(i, i ^ k) for i in range(size)])


def exchange_chips(parts):
    return [parts[0]] + [xor_permute(parts[k], "table", CORES * k) for k in range(1, len(parts))]


def exchange_cores(parts):
    return [item for part in parts for item in (part, sibling(part))]


def exchange_whole(parts):
    height = parts[0].shape[0] // CORES
    stacked = jnp.stack(parts).reshape(len(parts) * CORES, height, parts[0].shape[1])
    moved = lax.all_to_all(stacked, "table", split_axis=0, concat_axis=0, tiled=True)
    moved = moved.reshape(len(parts), CORES * height, parts[0].shape[1])
    return [moved[r // CORES] for r in range(len(parts) * CORES)]


def permute(value, target):
    nodes, tables = lax.axis_size("node"), lax.axis_size("table")
    pairs = []
    for n in range(nodes):
        for t in range(tables):
            m, s = target(n, t)
            pairs.append((n * tables + t, m * tables + s))
    return lax.ppermute(value, ("node", "table"), pairs)


def near(value):
    return permute(value, lambda n, t: (n ^ (1 + t % 2), t))


def far(value):
    return permute(value, lambda n, t: (n ^ (2 - t % 2), t))


def across(value):
    return permute(value, lambda n, t: (n ^ 3 * (t % 2), t))


def sibling(value):
    return permute(value, lambda n, t: (n, t ^ 1))


def half_of(shard):
    half = shard.shape[0] // 2
    core = lax.axis_index("table") % 2
    return lax.dynamic_slice(shard, (core * half, 0), (half, shard.shape[1]))


def assemble(shard, first, first_other, second, second_other):
    node = lax.axis_index("node")
    core = lax.axis_index("table") % 2
    rows, width = shard.shape
    half = rows // 2
    whole = jnp.zeros((rows * lax.axis_size("node"), width), shard.dtype)
    for piece, row in (
        (shard, node * rows),
        (first, (node ^ (1 + core)) * rows),
        (first_other, (node ^ (2 - core)) * rows),
        (second, (node ^ 3) * rows + core * half),
        (second_other, (node ^ 3) * rows + (1 - core) * half),
    ):
        whole = lax.dynamic_update_slice(whole, piece, (row, 0))
    return whole


def body(emb_rows, tile_mult, tile_rows, tile_table, tile_slot, dense, cross_v, cross_u, cross_bias, cotangent):
    nodes, tables = lax.axis_size("node"), lax.axis_size("table")
    tiles, size = tile_mult.shape[0], tile_mult.shape[1]
    quota = tiles // nodes
    samples, cross = cotangent.shape
    rank = cross_v.shape[1]
    relative = tables <= 8
    bias = cross_bias.reshape(1, cross)

    part = jax.ShapeDtypeStruct((quota * size + meta_rows(quota), 128), BF16)
    hbm = pl.BlockSpec(memory_space=pltpu.HBM)
    parts = pl.pallas_call(
        functools.partial(products_kernel, quota, size),
        out_shape=[part] * 5,
        in_specs=[hbm] * 5,
        out_specs=[VMEM] * 5,
        scratch_shapes=[
            pltpu.SMEM((tiles,), jnp.int32),
            pltpu.SMEM((tiles,), jnp.int32),
            pltpu.SMEM((tiles,), jnp.int32),
            pltpu.VMEM(emb_rows.shape, BF16),
            pltpu.VMEM(tile_mult.shape, jnp.int32),
            pltpu.SemaphoreType.DMA((5,)),
        ],
        compiler_params=params(60),
        name="products",
    )(tile_rows, tile_table, tile_slot, emb_rows, tile_mult)
    first_v = near(cross_v)
    first_u = near(cross_u)
    own, far_out, opposite, hop_near, hop_opposite = parts
    parts = [
        own,
        far(far_out),
        sibling(far(sibling(hop_near))),
        across(opposite),
        sibling(across(sibling(hop_opposite))),
    ]
    second_v = far(half_of(first_v))
    first_u, first_v = lax.optimization_barrier((first_u, first_v))
    other_v = sibling(first_v)
    second_u = far(half_of(first_u))

    chips = tables // CORES
    listed = jax.ShapeDtypeStruct((CORES * (LIST * size + META), 128), BF16)
    *lists, index = pl.pallas_call(
        functools.partial(relay_kernel, quota, size, tables, relative),
        out_shape=[listed] * chips + [jax.ShapeDtypeStruct((tiles,), jnp.int32)],
        in_specs=[VMEM] * 5,
        out_specs=[VMEM] * chips + [SMEM],
        scratch_shapes=[
            pltpu.VMEM((tables * LIST, size, 128), F32),
            pltpu.SMEM((tables,), jnp.int32),
            pltpu.SMEM((tables * LIST,), jnp.int32),
        ],
        compiler_params=params(32),
        cost_estimate=pl.CostEstimate(flops=RELAY_FLOPS, bytes_accessed=0, transcendentals=0),
        name="relay",
    )(*parts)
    swap_u = first_u
    if relative:
        arrived = exchange_chips(lists)
        second_v, swap_u, *arrived = lax.optimization_barrier((second_v, first_u, *arrived))
        arrived = exchange_cores(arrived)
    else:
        arrived = exchange_whole(lists)
    full_v = assemble(cross_v, first_v, other_v, second_v, sibling(second_v))

    grad = jax.ShapeDtypeStruct((CORES * LIST * size, 128), BF16)
    first, scaled, slots, hidden = pl.pallas_call(
        functools.partial(pool_kernel, tables, size),
        out_shape=[
            jax.ShapeDtypeStruct((samples, cross), BF16),
            jax.ShapeDtypeStruct((samples, cross), BF16),
            jax.ShapeDtypeStruct((tables * LIST,), jnp.int32),
            jax.ShapeDtypeStruct((samples, rank), BF16),
        ],
        in_specs=[VMEM] * (tables + 3),
        out_specs=[VMEM, VMEM, SMEM, VMEM],
        scratch_shapes=[pltpu.VMEM((BAG_BLOCKS + 1, size, 128), F32)],
        compiler_params=params(24),
        name="pool",
    )(*arrived, dense, cotangent, full_v)

    if relative:
        second_u, scaled = lax.optimization_barrier((second_u, scaled))
    full_u = assemble(cross_u, first_u, sibling(swap_u), second_u, sibling(second_u))

    half = chips // 2
    groups = (range(half, chips), range(half))
    *far_grads, dhidden = pl.pallas_call(
        functools.partial(owner_kernel, groups[0], size),
        out_shape=[grad] * len(groups[0]) + [jax.ShapeDtypeStruct((samples, rank), BF16)],
        in_specs=[SMEM] + [VMEM] * 6,
        out_specs=[VMEM] * (len(groups[0]) + 1),
        compiler_params=params(24),
        name="owner",
    )(slots, hidden, scaled, full_v, full_u, bias, cotangent)
    near_grads = pl.pallas_call(
        functools.partial(blocks_kernel, groups[1], size),
        out_shape=[grad] * len(groups[1]),
        in_specs=[SMEM] + [VMEM] * 6,
        out_specs=[VMEM] * len(groups[1]),
        compiler_params=params(24),
        name="blocks",
    )(slots, hidden, dhidden, full_v, full_u, bias, cotangent)
    grads = [*near_grads, *far_grads]

    cross_out = pl.pallas_call(
        cross_kernel,
        out_shape=jax.ShapeDtypeStruct((samples, cross), BF16),
        in_specs=[VMEM] * 4,
        out_specs=VMEM,
        compiler_params=params(32),
        cost_estimate=pl.CostEstimate(
            flops=2 * samples * rank * cross, bytes_accessed=4 * samples * cross + 2 * rank * cross, transcendentals=0
        ),
        name="cross",
    )(first, hidden, full_u, bias)

    if relative:
        returned = exchange_chips(grads)
        returned[-1], cross_out = lax.optimization_barrier((returned[-1], cross_out))
        returned = exchange_cores(returned)
    else:
        returned = exchange_whole(grads)

    back = jax.ShapeDtypeStruct((quota * size, 128), BF16)
    backs = pl.pallas_call(
        functools.partial(return_kernel, nodes, quota, size, tables),
        out_shape=[back] * nodes,
        in_specs=[SMEM] + [VMEM] * tables,
        out_specs=[VMEM] * nodes,
        scratch_shapes=[pltpu.VMEM((tables * LIST, size, 128), BF16)],
        compiler_params=params(32),
        name="back",
    )(index, *returned)
    backs = [backs[0]] + [xor_permute(backs[k], "node", k) for k in range(1, nodes)]

    emb_grad = pl.pallas_call(
        functools.partial(rows_kernel, nodes, quota, size),
        out_shape=jax.ShapeDtypeStruct(emb_rows.shape, F32),
        in_specs=[SMEM] + [VMEM] * (nodes + 1),
        out_specs=VMEM,
        compiler_params=params(16),
        name="rows",
    )(tile_rows, tile_mult, *backs)
    return cross_out, emb_grad


def solution(mesh):
    both = ("node", "table")
    in_specs = (
        P(both, None),
        P(both, None, None),
        P(both),
        P(both),
        P(both),
        P(both, None),
        P("node", None),
        P("node", None),
        P(),
        P(both, None),
    )
    out_specs = (P(both, None), P(both, None))
    return jax.shard_map(body, mesh=mesh, in_specs=in_specs, out_specs=out_specs, check_vma=False)
```

```python
import functools

import jax
import jax.numpy as jnp
from jax import lax
from jax.experimental import pallas as pl
from jax.experimental.pallas import tpu as pltpu
from jax.sharding import PartitionSpec as P

FEATURES = 26
SAMPLE_BLOCKS = 2
BAG_BLOCKS = 52
CORES = 2
LIST = 2
META = 16
RELAY_FLOPS = 10**6
BF16 = jnp.bfloat16
F32 = jnp.float32
SMEM = pl.BlockSpec(memory_space=pltpu.SMEM)
VMEM = pl.BlockSpec(memory_space=pltpu.VMEM)


def params(mib):
    return pltpu.CompilerParams(vmem_limit_bytes=mib << 20)


def nt_dot(left, right):
    return lax.dot_general(left, right, (((1,), (1,)), ((), ())), preferred_element_type=F32)


def tn_dot(left, right):
    return lax.dot_general(left, right, (((0,), (0,)), ((), ())), preferred_element_type=F32)


def dot(left, right):
    return jnp.dot(left, right, preferred_element_type=F32)


def block(index, size):
    return pl.ds(pl.multiple_of(index * size, size), size)


def meta_rows(count):
    return -(-2 * count // 16) * 16


def id_rows(values, rows):
    row = lax.broadcasted_iota(jnp.int32, (rows, 128), 0)
    filled = jnp.full((rows, 128), -1.0, F32)
    for i, value in enumerate(values):
        filled = jnp.where(row == i, value.astype(F32), filled)
    return filled.astype(BF16)


def swap_bits(core):
    return 1 + core, 2 - core


def products_kernel(quota, size, rows_hbm, table_hbm, slot_hbm, emb_hbm, mult_hbm, *refs):
    outs = refs[:5]
    rows_ref, table_ref, slot_ref, emb_ref, mult_ref, sems = refs[5:]
    pairs = ((mult_hbm, mult_ref), (emb_hbm, emb_ref), (rows_hbm, rows_ref), (table_hbm, table_ref), (slot_hbm, slot_ref))
    copies = [pltpu.make_async_copy(src, dst, sems.at[i]) for i, (src, dst) in enumerate(pairs)]
    for copy in copies:
        copy.start()
    for copy in copies:
        copy.wait()
    node = lax.axis_index("node")
    near_bit, far_bit = swap_bits(lax.axis_index("table") % CORES)
    own, far_out, opposite, hop_near, hop_opposite = outs
    for out, k in ((far_out, far_bit), (hop_near, near_bit), (opposite, 3), (own, 0)):
        ids = []
        for i in range(quota):
            tile = (node ^ k) * quota + i
            weights = mult_ref[tile].astype(F32).astype(BF16)
            part = dot(weights, emb_ref[block(rows_ref[tile], size), :])
            out[i * size : (i + 1) * size, :] = part.astype(BF16)
            ids += [table_ref[tile], slot_ref[tile]]
        out[quota * size :, :] = id_rows(ids, meta_rows(quota))
    hop_opposite[...] = opposite[...]


def relay_kernel(quota, size, tables, relative, *refs):
    chips = tables // CORES
    own, by_far, by_near, opposite, opposite_hop = refs[:5]
    outs = refs[5 : 5 + chips]
    index_ref, total, first_slot, slots = refs[5 + chips :]
    table = lax.axis_index("table")
    for r in range(tables):
        first_slot[r] = -1
        for e in range(LIST):
            slots[r * LIST + e] = -1
            total[r * LIST + e] = jnp.zeros((size, 128), F32)
    core = table % CORES
    near_bit, far_bit = swap_bits(core)

    def rows_of(part, rows):
        if part is opposite:
            return jnp.where(core == 1, opposite[rows, :].astype(F32), opposite_hop[rows, :].astype(F32))
        return part[rows, :].astype(F32)

    for part, k in ((own, 0), (by_far, far_bit), (by_near, near_bit), (opposite, 3)):
        ids = rows_of(part, slice(quota * size, None)).astype(jnp.int32)
        for i in range(quota):
            target, slot = ids[2 * i, 0], ids[2 * i + 1, 0]
            entry = target ^ table if relative else target
            known = first_slot[entry]
            which = jnp.where((known < 0) | (known == slot), 0, 1)
            first_slot[entry] = jnp.where(known < 0, slot, known)
            place = entry * LIST + which
            slots[place] = slot
            index_ref[k * quota + i] = place
            total[place] += rows_of(part, slice(i * size, (i + 1) * size))
    for r in range(tables):
        out, base = outs[r // CORES], r % CORES * (LIST * size + META)
        for e in range(LIST):
            out[base + e * size : base + (e + 1) * size, :] = total[r * LIST + e].astype(BF16)
        base += LIST * size
        out[base : base + META, :] = id_rows([slots[r * LIST + e] for e in range(LIST)], META)


def pool_kernel(tables, size, *refs):
    parts = refs[:tables]
    dense_ref, cot_ref, v_ref, first_ref, scaled_ref, slot_ref, hidden_ref, total = refs[tables:]
    for b in range(BAG_BLOCKS + 1):
        total[b] = jnp.zeros((size, 128), F32)
    for r in range(tables):
        part, base = parts[r], r % CORES * (LIST * size + META)
        ids = part[base + LIST * size : base + LIST * size + META, :].astype(F32).astype(jnp.int32)
        for e in range(LIST):
            slot_ref[r * LIST + e] = ids[e, 0]
            begin = base + e * size
            place = jnp.where(ids[e, 0] < 0, BAG_BLOCKS, ids[e, 0])
            total[place] += part[begin : begin + size, :].astype(F32)

    first_ref[:, :128] = dense_ref[...]
    for f in range(FEATURES):
        for s in range(SAMPLE_BLOCKS):
            columns = slice((f + 1) * 128, (f + 2) * 128)
            first_ref[s * size : (s + 1) * size, columns] = total[f * SAMPLE_BLOCKS + s].astype(BF16)
    hidden_ref[...] = dot(first_ref[...], v_ref[...]).astype(BF16)
    for f in range(FEATURES + 1):
        columns = slice(f * 128, (f + 1) * 128)
        scaled_ref[:, columns] = (cot_ref[:, columns].astype(F32) * first_ref[:, columns].astype(F32)).astype(BF16)


def blocks_kernel(group, size, slot_ref, hidden_ref, dhidden_ref, v_ref, u_ref, bias_ref, cot_ref, *outs):
    for chip, out in zip(group, outs):
        for entry in range(CORES * LIST):
            slot = jnp.maximum(slot_ref[chip * CORES * LIST + entry], 0)
            columns = block(slot // SAMPLE_BLOCKS + 1, 128)
            samples = block(slot % SAMPLE_BLOCKS, size)
            scale = dot(hidden_ref[samples, :], u_ref[:, columns]) + bias_ref[:, columns]
            grad = cot_ref[samples, columns].astype(F32) * (scale + 1.0)
            grad = grad + nt_dot(dhidden_ref[samples, :], v_ref[columns, :])
            out[entry * size : (entry + 1) * size, :] = grad.astype(BF16)


def owner_kernel(group, size, slot_ref, hidden_ref, scaled_ref, v_ref, u_ref, bias_ref, cot_ref, *outs):
    dhidden_ref = outs[-1]
    dhidden_ref[...] = nt_dot(scaled_ref[...], u_ref[...]).astype(BF16)
    blocks_kernel(group, size, slot_ref, hidden_ref, dhidden_ref, v_ref, u_ref, bias_ref, cot_ref, *outs[:-1])


def cross_kernel(first_ref, hidden_ref, u_ref, bias_ref, out_ref):
    width = first_ref.shape[1]
    step = 256
    for start in range(0, width, step):
        columns = slice(start, min(start + step, width))
        scale = dot(hidden_ref[...], u_ref[:, columns]) + bias_ref[:, columns]
        out_ref[:, columns] = (first_ref[:, columns].astype(F32) * (scale + 1.0)).astype(BF16)


def return_kernel(nodes, quota, size, tables, index_ref, *refs):
    parts, outs, staged = refs[:tables], refs[tables : tables + nodes], refs[-1]
    for r in range(tables):
        for e in range(LIST):
            begin = (r % CORES * LIST + e) * size
            staged[r * LIST + e] = parts[r][begin : begin + size, :]
    for k in range(nodes):
        for i in range(quota):
            outs[k][i * size : (i + 1) * size, :] = staged[index_ref[k * quota + i]]


def rows_kernel(nodes, quota, size, rows_ref, mult_ref, *refs):
    parts, out_ref = refs[:nodes], refs[nodes]
    node = lax.axis_index("node")
    out_ref[...] = jnp.zeros(out_ref.shape, F32)
    for k in range(nodes):
        for i in range(quota):
            tile = (node ^ k) * quota + i
            weights = mult_ref[tile].astype(F32).astype(BF16)
            rows = block(rows_ref[tile], size)
            out_ref[rows, :] += tn_dot(weights, parts[k][i * size : (i + 1) * size, :])


def xor_permute(value, axis, k):
    size = lax.axis_size(axis)
    return lax.ppermute(value, axis, [(i, i ^ k) for i in range(size)])


def exchange_chips(parts):
    arrived = list(parts)
    for k in range(1, len(parts)):
        arrived[k] = xor_permute(parts[k], "table", CORES * k)
    return arrived


def exchange_cores(parts):
    return [item for part in parts for item in (part, sibling(part))]


def exchange_whole(parts):
    height = parts[0].shape[0] // CORES
    stacked = jnp.stack(parts).reshape(len(parts) * CORES, height, parts[0].shape[1])
    moved = lax.all_to_all(stacked, "table", split_axis=0, concat_axis=0, tiled=True)
    moved = moved.reshape(len(parts), CORES * height, parts[0].shape[1])
    return [moved[r // CORES] for r in range(len(parts) * CORES)]


def permute(value, target):
    nodes, tables = lax.axis_size("node"), lax.axis_size("table")
    pairs = []
    for n in range(nodes):
        for t in range(tables):
            m, s = target(n, t)
            pairs.append((n * tables + t, m * tables + s))
    return lax.ppermute(value, ("node", "table"), pairs)


def near(value):
    return permute(value, lambda n, t: (n ^ (1 + t % 2), t))


def far(value):
    return permute(value, lambda n, t: (n ^ (2 - t % 2), t))


def across(value):
    return permute(value, lambda n, t: (n ^ 3 * (t % 2), t))


def sibling(value):
    return permute(value, lambda n, t: (n, t ^ 1))


def half_of(shard):
    half = shard.shape[0] // 2
    core = lax.axis_index("table") % 2
    return lax.dynamic_slice(shard, (core * half, 0), (half, shard.shape[1]))


def assemble(shard, first, first_other, second, second_other):
    node = lax.axis_index("node")
    core = lax.axis_index("table") % 2
    rows, width = shard.shape
    half = rows // 2
    whole = jnp.zeros((rows * lax.axis_size("node"), width), shard.dtype)
    for piece, row in (
        (shard, node * rows),
        (first, (node ^ (1 + core)) * rows),
        (first_other, (node ^ (2 - core)) * rows),
        (second, (node ^ 3) * rows + core * half),
        (second_other, (node ^ 3) * rows + (1 - core) * half),
    ):
        whole = lax.dynamic_update_slice(whole, piece, (row, 0))
    return whole


def body(emb_rows, tile_mult, tile_rows, tile_table, tile_slot, dense, cross_v, cross_u, cross_bias, cotangent):
    nodes, tables = lax.axis_size("node"), lax.axis_size("table")
    tiles, size = tile_mult.shape[0], tile_mult.shape[1]
    quota = tiles // nodes
    samples, cross = cotangent.shape
    rank = cross_v.shape[1]
    relative = tables <= 8

    part = jax.ShapeDtypeStruct((quota * size + meta_rows(quota), 128), BF16)
    hbm = pl.BlockSpec(memory_space=pltpu.HBM)
    parts = pl.pallas_call(
        functools.partial(products_kernel, quota, size),
        out_shape=[part] * 5,
        in_specs=[hbm] * 5,
        out_specs=[VMEM] * 5,
        scratch_shapes=[
            pltpu.SMEM((tiles,), jnp.int32),
            pltpu.SMEM((tiles,), jnp.int32),
            pltpu.SMEM((tiles,), jnp.int32),
            pltpu.VMEM(emb_rows.shape, BF16),
            pltpu.VMEM(tile_mult.shape, jnp.int32),
            pltpu.SemaphoreType.DMA((5,)),
        ],
        compiler_params=params(60),
        name="products",
    )(tile_rows, tile_table, tile_slot, emb_rows, tile_mult)
    first_v = near(cross_v)
    first_u = near(cross_u)
    own, far_out, opposite, hop_near, hop_opposite = parts
    parts = [
        own,
        far(far_out),
        sibling(far(sibling(hop_near))),
        across(opposite),
        sibling(across(sibling(hop_opposite))),
    ]
    chips = tables // CORES
    listed = jax.ShapeDtypeStruct((CORES * (LIST * size + META), 128), BF16)
    *lists, index = pl.pallas_call(
        functools.partial(relay_kernel, quota, size, tables, relative),
        out_shape=[listed] * chips + [jax.ShapeDtypeStruct((tiles,), jnp.int32)],
        in_specs=[VMEM] * 5,
        out_specs=[VMEM] * chips + [SMEM],
        scratch_shapes=[
            pltpu.VMEM((tables * LIST, size, 128), F32),
            pltpu.SMEM((tables,), jnp.int32),
            pltpu.SMEM((tables * LIST,), jnp.int32),
        ],
        compiler_params=params(32),
        cost_estimate=pl.CostEstimate(flops=RELAY_FLOPS, bytes_accessed=0, transcendentals=0),
        name="relay",
    )(*parts)
    half_v = half_of(first_v)
    if relative:
        half_v, lists[1] = lax.optimization_barrier((half_v, lists[1]))
    second_v = far(half_v)
    first_u, first_v = lax.optimization_barrier((first_u, first_v))
    other_v = sibling(first_v)
    second_u = far(half_of(first_u))
    late_v, late_u, late_bias, lists[0] = lax.optimization_barrier((cross_v, cross_u, cross_bias, lists[0]))
    bias = late_bias.reshape(1, cross)
    swap_u = first_u
    if relative:
        arrived = exchange_chips(lists)
        second_v, swap_u, *arrived = lax.optimization_barrier((second_v, first_u, *arrived))
        arrived = exchange_cores(arrived)
    else:
        arrived = exchange_whole(lists)
    full_v = assemble(late_v, first_v, other_v, second_v, sibling(second_v))

    grad = jax.ShapeDtypeStruct((CORES * LIST * size, 128), BF16)
    first, scaled, slots, hidden = pl.pallas_call(
        functools.partial(pool_kernel, tables, size),
        out_shape=[
            jax.ShapeDtypeStruct((samples, cross), BF16),
            jax.ShapeDtypeStruct((samples, cross), BF16),
            jax.ShapeDtypeStruct((tables * LIST,), jnp.int32),
            jax.ShapeDtypeStruct((samples, rank), BF16),
        ],
        in_specs=[VMEM] * (tables + 3),
        out_specs=[VMEM, VMEM, SMEM, VMEM],
        scratch_shapes=[pltpu.VMEM((BAG_BLOCKS + 1, size, 128), F32)],
        compiler_params=params(24),
        name="pool",
    )(*arrived, dense, cotangent, full_v)

    if relative:
        second_u, scaled = lax.optimization_barrier((second_u, scaled))
    full_u = assemble(late_u, first_u, sibling(swap_u), second_u, sibling(second_u))

    half = chips // 2
    groups = (range(half, chips), range(half))
    *far_grads, dhidden = pl.pallas_call(
        functools.partial(owner_kernel, groups[0], size),
        out_shape=[grad] * len(groups[0]) + [jax.ShapeDtypeStruct((samples, rank), BF16)],
        in_specs=[SMEM] + [VMEM] * 6,
        out_specs=[VMEM] * (len(groups[0]) + 1),
        compiler_params=params(24),
        name="owner",
    )(slots, hidden, scaled, full_v, full_u, bias, cotangent)
    near_grads = pl.pallas_call(
        functools.partial(blocks_kernel, groups[1], size),
        out_shape=[grad] * len(groups[1]),
        in_specs=[SMEM] + [VMEM] * 6,
        out_specs=[VMEM] * len(groups[1]),
        compiler_params=params(24),
        name="blocks",
    )(slots, hidden, dhidden, full_v, full_u, bias, cotangent)
    grads = [*near_grads, *far_grads]

    cross_out = pl.pallas_call(
        cross_kernel,
        out_shape=jax.ShapeDtypeStruct((samples, cross), BF16),
        in_specs=[VMEM] * 4,
        out_specs=VMEM,
        compiler_params=params(32),
        cost_estimate=pl.CostEstimate(
            flops=2 * samples * rank * cross, bytes_accessed=4 * samples * cross + 2 * rank * cross, transcendentals=0
        ),
        name="cross",
    )(first, hidden, full_u, bias)

    if relative:
        returned = exchange_chips(grads)
        returned[-1], cross_out = lax.optimization_barrier((returned[-1], cross_out))
        returned = exchange_cores(returned)
    else:
        returned = exchange_whole(grads)

    back = jax.ShapeDtypeStruct((quota * size, 128), BF16)
    backs = pl.pallas_call(
        functools.partial(return_kernel, nodes, quota, size, tables),
        out_shape=[back] * nodes,
        in_specs=[SMEM] + [VMEM] * tables,
        out_specs=[VMEM] * nodes,
        scratch_shapes=[pltpu.VMEM((tables * LIST, size, 128), BF16)],
        compiler_params=params(32),
        name="back",
    )(index, *returned)
    backs = list(backs)
    for k in range(1, nodes):
        backs[k] = xor_permute(backs[k], "node", k)

    emb_grad = pl.pallas_call(
        functools.partial(rows_kernel, nodes, quota, size),
        out_shape=jax.ShapeDtypeStruct(emb_rows.shape, F32),
        in_specs=[SMEM] + [VMEM] * (nodes + 1),
        out_specs=VMEM,
        compiler_params=params(16),
        name="rows",
    )(tile_rows, tile_mult, *backs)
    return cross_out, emb_grad


def solution(mesh):
    both = ("node", "table")
    in_specs = (
        P(both, None),
        P(both, None, None),
        P(both),
        P(both),
        P(both),
        P(both, None),
        P("node", None),
        P("node", None),
        P(),
        P(both, None),
    )
    out_specs = (P(both, None), P(both, None))
    return jax.shard_map(body, mesh=mesh, in_specs=in_specs, out_specs=out_specs, check_vma=False)
```

```python
import functools

import jax
import jax.numpy as jnp
from jax import lax
from jax.experimental import pallas as pl
from jax.experimental.pallas import tpu as pltpu
from jax.sharding import PartitionSpec as P

FEATURES = 26
SAMPLE_BLOCKS = 2
BAG_BLOCKS = 52
CORES = 2
LIST = 2
META = 16
RELAY_FLOPS = 10**6
BF16 = jnp.bfloat16
F32 = jnp.float32
SMEM = pl.BlockSpec(memory_space=pltpu.SMEM)
VMEM = pl.BlockSpec(memory_space=pltpu.VMEM)


def params(mib):
    return pltpu.CompilerParams(vmem_limit_bytes=mib << 20)


def nt_dot(left, right):
    return lax.dot_general(left, right, (((1,), (1,)), ((), ())), preferred_element_type=F32)


def tn_dot(left, right):
    return lax.dot_general(left, right, (((0,), (0,)), ((), ())), preferred_element_type=F32)


def dot(left, right):
    return jnp.dot(left, right, preferred_element_type=F32)


def block(index, size):
    return pl.ds(pl.multiple_of(index * size, size), size)


def meta_rows(count):
    return -(-2 * count // 16) * 16


def id_rows(values, rows):
    row = lax.broadcasted_iota(jnp.int32, (rows, 128), 0)
    filled = jnp.full((rows, 128), -1.0, F32)
    for i, value in enumerate(values):
        filled = jnp.where(row == i, value.astype(F32), filled)
    return filled.astype(BF16)


def swap_bits(core):
    return 1 + core, 2 - core


def products_kernel(quota, size, rows_hbm, table_hbm, slot_hbm, emb_hbm, mult_hbm, *refs):
    outs = refs[:5]
    rows_ref, table_ref, slot_ref, emb_ref, mult_ref, sems = refs[5:]
    pairs = ((mult_hbm, mult_ref), (emb_hbm, emb_ref), (rows_hbm, rows_ref), (table_hbm, table_ref), (slot_hbm, slot_ref))
    copies = [pltpu.make_async_copy(src, dst, sems.at[i]) for i, (src, dst) in enumerate(pairs)]
    for copy in copies:
        copy.start()
    for copy in copies:
        copy.wait()
    node = lax.axis_index("node")
    near_bit, far_bit = swap_bits(lax.axis_index("table") % CORES)
    own, far_out, opposite, hop_near, hop_opposite = outs
    for out, k in ((far_out, far_bit), (hop_near, near_bit), (opposite, 3), (own, 0)):
        ids = []
        for i in range(quota):
            tile = (node ^ k) * quota + i
            weights = mult_ref[tile].astype(F32).astype(BF16)
            part = dot(weights, emb_ref[block(rows_ref[tile], size), :])
            out[i * size : (i + 1) * size, :] = part.astype(BF16)
            ids += [table_ref[tile], slot_ref[tile]]
        out[quota * size :, :] = id_rows(ids, meta_rows(quota))
    hop_opposite[...] = opposite[...]


def relay_kernel(quota, size, tables, relative, *refs):
    chips = tables // CORES
    own, by_far, by_near, opposite, opposite_hop = refs[:5]
    outs = refs[5 : 5 + chips]
    index_ref, total, first_slot, slots = refs[5 + chips :]
    table = lax.axis_index("table")
    for r in range(tables):
        first_slot[r] = -1
        for e in range(LIST):
            slots[r * LIST + e] = -1
            total[r * LIST + e] = jnp.zeros((size, 128), F32)
    core = table % CORES
    near_bit, far_bit = swap_bits(core)

    def rows_of(part, rows):
        if part is opposite:
            return jnp.where(core == 1, opposite[rows, :].astype(F32), opposite_hop[rows, :].astype(F32))
        return part[rows, :].astype(F32)

    for part, k in ((own, 0), (by_far, far_bit), (by_near, near_bit), (opposite, 3)):
        ids = rows_of(part, slice(quota * size, None)).astype(jnp.int32)
        for i in range(quota):
            target, slot = ids[2 * i, 0], ids[2 * i + 1, 0]
            entry = target ^ table if relative else target
            known = first_slot[entry]
            which = jnp.where((known < 0) | (known == slot), 0, 1)
            first_slot[entry] = jnp.where(known < 0, slot, known)
            place = entry * LIST + which
            slots[place] = slot
            index_ref[k * quota + i] = place
            total[place] += rows_of(part, slice(i * size, (i + 1) * size))
    for r in range(tables):
        out, base = outs[r // CORES], r % CORES * (LIST * size + META)
        for e in range(LIST):
            out[base + e * size : base + (e + 1) * size, :] = total[r * LIST + e].astype(BF16)
        base += LIST * size
        out[base : base + META, :] = id_rows([slots[r * LIST + e] for e in range(LIST)], META)


def pool_kernel(tables, size, *refs):
    parts = refs[:tables]
    dense_ref, cot_ref, v_ref, first_ref, scaled_ref, slot_ref, hidden_ref, total = refs[tables:]
    for b in range(BAG_BLOCKS + 1):
        total[b] = jnp.zeros((size, 128), F32)
    for r in range(tables):
        part, base = parts[r], r % CORES * (LIST * size + META)
        ids = part[base + LIST * size : base + LIST * size + META, :].astype(F32).astype(jnp.int32)
        for e in range(LIST):
            slot_ref[r * LIST + e] = ids[e, 0]
            begin = base + e * size
            place = jnp.where(ids[e, 0] < 0, BAG_BLOCKS, ids[e, 0])
            total[place] += part[begin : begin + size, :].astype(F32)

    first_ref[:, :128] = dense_ref[...]
    for f in range(FEATURES):
        for s in range(SAMPLE_BLOCKS):
            columns = slice((f + 1) * 128, (f + 2) * 128)
            first_ref[s * size : (s + 1) * size, columns] = total[f * SAMPLE_BLOCKS + s].astype(BF16)
    hidden_ref[...] = dot(first_ref[...], v_ref[...]).astype(BF16)
    for f in range(FEATURES + 1):
        columns = slice(f * 128, (f + 1) * 128)
        scaled_ref[:, columns] = (cot_ref[:, columns].astype(F32) * first_ref[:, columns].astype(F32)).astype(BF16)


def blocks_kernel(group, size, slot_ref, hidden_ref, dhidden_ref, v_ref, u_ref, bias_ref, cot_ref, *outs):
    for chip, out in zip(group, outs):
        for entry in range(CORES * LIST):
            slot = jnp.maximum(slot_ref[chip * CORES * LIST + entry], 0)
            columns = block(slot // SAMPLE_BLOCKS + 1, 128)
            samples = block(slot % SAMPLE_BLOCKS, size)
            scale = dot(hidden_ref[samples, :], u_ref[:, columns]) + bias_ref[:, columns]
            grad = cot_ref[samples, columns].astype(F32) * (scale + 1.0)
            grad = grad + nt_dot(dhidden_ref[samples, :], v_ref[columns, :])
            out[entry * size : (entry + 1) * size, :] = grad.astype(BF16)


def owner_kernel(group, size, slot_ref, hidden_ref, scaled_ref, v_ref, u_ref, bias_ref, cot_ref, *outs):
    dhidden_ref = outs[-1]
    dhidden_ref[...] = nt_dot(scaled_ref[...], u_ref[...]).astype(BF16)
    blocks_kernel(group, size, slot_ref, hidden_ref, dhidden_ref, v_ref, u_ref, bias_ref, cot_ref, *outs[:-1])


def cross_kernel(first_ref, hidden_ref, u_ref, bias_ref, out_ref):
    width = first_ref.shape[1]
    step = 256
    for start in range(0, width, step):
        columns = slice(start, min(start + step, width))
        scale = dot(hidden_ref[...], u_ref[:, columns]) + bias_ref[:, columns]
        out_ref[:, columns] = (first_ref[:, columns].astype(F32) * (scale + 1.0)).astype(BF16)


def return_kernel(nodes, quota, size, tables, index_ref, *refs):
    parts, outs, staged = refs[:tables], refs[tables : tables + nodes], refs[-1]
    for r in range(tables):
        for e in range(LIST):
            begin = (r % CORES * LIST + e) * size
            staged[r * LIST + e] = parts[r][begin : begin + size, :]
    for k in range(nodes):
        for i in range(quota):
            outs[k][i * size : (i + 1) * size, :] = staged[index_ref[k * quota + i]]


def rows_kernel(nodes, quota, size, rows_ref, mult_ref, *refs):
    parts, out_ref = refs[:nodes], refs[nodes]
    node = lax.axis_index("node")
    out_ref[...] = jnp.zeros(out_ref.shape, F32)
    for k in range(nodes):
        for i in range(quota):
            tile = (node ^ k) * quota + i
            weights = mult_ref[tile].astype(F32).astype(BF16)
            rows = block(rows_ref[tile], size)
            out_ref[rows, :] += tn_dot(weights, parts[k][i * size : (i + 1) * size, :])


def xor_permute(value, axis, k):
    size = lax.axis_size(axis)
    return lax.ppermute(value, axis, [(i, i ^ k) for i in range(size)])


def exchange_chips(parts):
    arrived = list(parts)
    for k in range(1, len(parts)):
        arrived[k] = xor_permute(parts[k], "table", CORES * k)
    return arrived


def exchange_cores(parts):
    return [item for part in parts for item in (part, sibling(part))]


def exchange_whole(parts):
    height = parts[0].shape[0] // CORES
    stacked = jnp.stack(parts).reshape(len(parts) * CORES, height, parts[0].shape[1])
    moved = lax.all_to_all(stacked, "table", split_axis=0, concat_axis=0, tiled=True)
    moved = moved.reshape(len(parts), CORES * height, parts[0].shape[1])
    return [moved[r // CORES] for r in range(len(parts) * CORES)]


def permute(value, target):
    nodes, tables = lax.axis_size("node"), lax.axis_size("table")
    pairs = []
    for n in range(nodes):
        for t in range(tables):
            m, s = target(n, t)
            pairs.append((n * tables + t, m * tables + s))
    return lax.ppermute(value, ("node", "table"), pairs)


def near(value):
    return permute(value, lambda n, t: (n ^ (1 + t % 2), t))


def far(value):
    return permute(value, lambda n, t: (n ^ (2 - t % 2), t))


def across(value):
    return permute(value, lambda n, t: (n ^ 3 * (t % 2), t))


def sibling(value):
    return permute(value, lambda n, t: (n, t ^ 1))


def half_of(shard):
    half = shard.shape[0] // 2
    core = lax.axis_index("table") % 2
    return lax.dynamic_slice(shard, (core * half, 0), (half, shard.shape[1]))


def assemble(shard, first, first_other, second, second_other):
    node = lax.axis_index("node")
    core = lax.axis_index("table") % 2
    rows, width = shard.shape
    half = rows // 2
    whole = jnp.zeros((rows * lax.axis_size("node"), width), shard.dtype)
    for piece, row in (
        (shard, node * rows),
        (first, (node ^ (1 + core)) * rows),
        (first_other, (node ^ (2 - core)) * rows),
        (second, (node ^ 3) * rows + core * half),
        (second_other, (node ^ 3) * rows + (1 - core) * half),
    ):
        whole = lax.dynamic_update_slice(whole, piece, (row, 0))
    return whole


def body(emb_rows, tile_mult, tile_rows, tile_table, tile_slot, dense, cross_v, cross_u, cross_bias, cotangent):
    nodes, tables = lax.axis_size("node"), lax.axis_size("table")
    tiles, size = tile_mult.shape[0], tile_mult.shape[1]
    quota = tiles // nodes
    samples, cross = cotangent.shape
    rank = cross_v.shape[1]
    relative = tables <= 8

    part = jax.ShapeDtypeStruct((quota * size + meta_rows(quota), 128), BF16)
    hbm = pl.BlockSpec(memory_space=pltpu.HBM)
    parts = pl.pallas_call(
        functools.partial(products_kernel, quota, size),
        out_shape=[part] * 5,
        in_specs=[hbm] * 5,
        out_specs=[VMEM] * 5,
        scratch_shapes=[
            pltpu.SMEM((tiles,), jnp.int32),
            pltpu.SMEM((tiles,), jnp.int32),
            pltpu.SMEM((tiles,), jnp.int32),
            pltpu.VMEM(emb_rows.shape, BF16),
            pltpu.VMEM(tile_mult.shape, jnp.int32),
            pltpu.SemaphoreType.DMA((5,)),
        ],
        compiler_params=params(60),
        name="products",
    )(tile_rows, tile_table, tile_slot, emb_rows, tile_mult)
    first_v = near(cross_v)
    first_u = near(cross_u)
    own, far_out, opposite, hop_near, hop_opposite = parts
    parts = [
        own,
        far(far_out),
        sibling(far(sibling(hop_near))),
        across(opposite),
        sibling(across(sibling(hop_opposite))),
    ]
    chips = tables // CORES
    listed = jax.ShapeDtypeStruct((CORES * (LIST * size + META), 128), BF16)
    *lists, index = pl.pallas_call(
        functools.partial(relay_kernel, quota, size, tables, relative),
        out_shape=[listed] * chips + [jax.ShapeDtypeStruct((tiles,), jnp.int32)],
        in_specs=[VMEM] * 5,
        out_specs=[VMEM] * chips + [SMEM],
        scratch_shapes=[
            pltpu.VMEM((tables * LIST, size, 128), F32),
            pltpu.SMEM((tables,), jnp.int32),
            pltpu.SMEM((tables * LIST,), jnp.int32),
        ],
        compiler_params=params(32),
        cost_estimate=pl.CostEstimate(flops=RELAY_FLOPS, bytes_accessed=0, transcendentals=0),
        name="relay",
    )(*parts)
    half_v = half_of(first_v)
    if relative:
        half_v, lists[1] = lax.optimization_barrier((half_v, lists[1]))
    second_v = far(half_v)
    first_u, first_v, late_v, late_u, late_bias = lax.optimization_barrier(
        (first_u, first_v, cross_v, cross_u, cross_bias)
    )
    other_v = sibling(first_v)
    second_u = far(half_of(first_u))
    bias = late_bias.reshape(1, cross)
    swap_u = first_u
    if relative:
        arrived = exchange_chips(lists)
        second_v, swap_u, *arrived = lax.optimization_barrier((second_v, first_u, *arrived))
        arrived = exchange_cores(arrived)
    else:
        arrived = exchange_whole(lists)
    full_v = assemble(late_v, first_v, other_v, second_v, sibling(second_v))

    grad = jax.ShapeDtypeStruct((CORES * LIST * size, 128), BF16)
    first, scaled, slots, hidden = pl.pallas_call(
        functools.partial(pool_kernel, tables, size),
        out_shape=[
            jax.ShapeDtypeStruct((samples, cross), BF16),
            jax.ShapeDtypeStruct((samples, cross), BF16),
            jax.ShapeDtypeStruct((tables * LIST,), jnp.int32),
            jax.ShapeDtypeStruct((samples, rank), BF16),
        ],
        in_specs=[VMEM] * (tables + 3),
        out_specs=[VMEM, VMEM, SMEM, VMEM],
        scratch_shapes=[pltpu.VMEM((BAG_BLOCKS + 1, size, 128), F32)],
        compiler_params=params(24),
        name="pool",
    )(*arrived, dense, cotangent, full_v)

    if relative:
        second_u, scaled = lax.optimization_barrier((second_u, scaled))
    full_u = assemble(late_u, first_u, sibling(swap_u), second_u, sibling(second_u))

    half = chips // 2
    groups = (range(half, chips), range(half))
    *far_grads, dhidden = pl.pallas_call(
        functools.partial(owner_kernel, groups[0], size),
        out_shape=[grad] * len(groups[0]) + [jax.ShapeDtypeStruct((samples, rank), BF16)],
        in_specs=[SMEM] + [VMEM] * 6,
        out_specs=[VMEM] * (len(groups[0]) + 1),
        compiler_params=params(24),
        name="owner",
    )(slots, hidden, scaled, full_v, full_u, bias, cotangent)
    near_grads = pl.pallas_call(
        functools.partial(blocks_kernel, groups[1], size),
        out_shape=[grad] * len(groups[1]),
        in_specs=[SMEM] + [VMEM] * 6,
        out_specs=[VMEM] * len(groups[1]),
        compiler_params=params(24),
        name="blocks",
    )(slots, hidden, dhidden, full_v, full_u, bias, cotangent)
    grads = [*near_grads, *far_grads]

    cross_out = pl.pallas_call(
        cross_kernel,
        out_shape=jax.ShapeDtypeStruct((samples, cross), BF16),
        in_specs=[VMEM] * 4,
        out_specs=VMEM,
        compiler_params=params(32),
        cost_estimate=pl.CostEstimate(
            flops=2 * samples * rank * cross, bytes_accessed=4 * samples * cross + 2 * rank * cross, transcendentals=0
        ),
        name="cross",
    )(first, hidden, full_u, bias)

    if relative:
        returned = exchange_chips(grads)
        returned[-1], cross_out = lax.optimization_barrier((returned[-1], cross_out))
        returned = exchange_cores(returned)
    else:
        returned = exchange_whole(grads)

    back = jax.ShapeDtypeStruct((quota * size, 128), BF16)
    backs = pl.pallas_call(
        functools.partial(return_kernel, nodes, quota, size, tables),
        out_shape=[back] * nodes,
        in_specs=[SMEM] + [VMEM] * tables,
        out_specs=[VMEM] * nodes,
        scratch_shapes=[pltpu.VMEM((tables * LIST, size, 128), BF16)],
        compiler_params=params(32),
        name="back",
    )(index, *returned)
    backs = list(backs)
    for k in range(1, nodes):
        backs[k] = xor_permute(backs[k], "node", k)

    emb_grad = pl.pallas_call(
        functools.partial(rows_kernel, nodes, quota, size),
        out_shape=jax.ShapeDtypeStruct(emb_rows.shape, F32),
        in_specs=[SMEM] + [VMEM] * (nodes + 1),
        out_specs=VMEM,
        compiler_params=params(16),
        name="rows",
    )(tile_rows, tile_mult, *backs)
    return cross_out, emb_grad


def solution(mesh):
    both = ("node", "table")
    in_specs = (
        P(both, None),
        P(both, None, None),
        P(both),
        P(both),
        P(both),
        P(both, None),
        P("node", None),
        P("node", None),
        P(),
        P(both, None),
    )
    out_specs = (P(both, None), P(both, None))
    return jax.shard_map(body, mesh=mesh, in_specs=in_specs, out_specs=out_specs, check_vma=False)
```

```python
import functools

import jax
import jax.numpy as jnp
from jax import lax
from jax.experimental import pallas as pl
from jax.experimental.pallas import tpu as pltpu
from jax.sharding import PartitionSpec as P

FEATURES = 26
SAMPLE_BLOCKS = 2
BAG_BLOCKS = 52
CORES = 2
LIST = 2
META = 16
RELAY_FLOPS = 10**6
BF16 = jnp.bfloat16
F32 = jnp.float32
SMEM = pl.BlockSpec(memory_space=pltpu.SMEM)
VMEM = pl.BlockSpec(memory_space=pltpu.VMEM)


def params(mib):
    return pltpu.CompilerParams(vmem_limit_bytes=mib << 20)


def nt_dot(left, right):
    return lax.dot_general(left, right, (((1,), (1,)), ((), ())), preferred_element_type=F32)


def tn_dot(left, right):
    return lax.dot_general(left, right, (((0,), (0,)), ((), ())), preferred_element_type=F32)


def dot(left, right):
    return jnp.dot(left, right, preferred_element_type=F32)


def block(index, size):
    return pl.ds(pl.multiple_of(index * size, size), size)


def meta_rows(count):
    return -(-2 * count // 16) * 16


def id_rows(values, rows):
    row = lax.broadcasted_iota(jnp.int32, (rows, 128), 0)
    filled = jnp.full((rows, 128), -1.0, F32)
    for i, value in enumerate(values):
        filled = jnp.where(row == i, value.astype(F32), filled)
    return filled.astype(BF16)


def swap_bits(core):
    return 1 + core, 2 - core


def products_kernel(quota, size, rows_hbm, table_hbm, slot_hbm, emb_hbm, mult_hbm, *refs):
    outs = refs[:5]
    rows_ref, table_ref, slot_ref, emb_ref, mult_ref, sems = refs[5:]
    pairs = ((mult_hbm, mult_ref), (emb_hbm, emb_ref), (rows_hbm, rows_ref), (table_hbm, table_ref), (slot_hbm, slot_ref))
    copies = [pltpu.make_async_copy(src, dst, sems.at[i]) for i, (src, dst) in enumerate(pairs)]
    for copy in copies:
        copy.start()
    for copy in copies:
        copy.wait()
    node = lax.axis_index("node")
    near_bit, far_bit = swap_bits(lax.axis_index("table") % CORES)
    own, far_out, opposite, hop_near, hop_opposite = outs
    for out, k in ((far_out, far_bit), (hop_near, near_bit), (opposite, 3), (own, 0)):
        ids = []
        for i in range(quota):
            tile = (node ^ k) * quota + i
            weights = mult_ref[tile].astype(F32).astype(BF16)
            part = dot(weights, emb_ref[block(rows_ref[tile], size), :])
            out[i * size : (i + 1) * size, :] = part.astype(BF16)
            ids += [table_ref[tile], slot_ref[tile]]
        out[quota * size :, :] = id_rows(ids, meta_rows(quota))
    hop_opposite[...] = opposite[...]


def relay_kernel(quota, size, tables, relative, *refs):
    chips = tables // CORES
    own, by_far, by_near, opposite, opposite_hop = refs[:5]
    outs = refs[5 : 5 + chips]
    index_ref, total, first_slot, slots = refs[5 + chips :]
    table = lax.axis_index("table")
    for r in range(tables):
        first_slot[r] = -1
        for e in range(LIST):
            slots[r * LIST + e] = -1
            total[r * LIST + e] = jnp.zeros((size, 128), F32)
    core = table % CORES
    near_bit, far_bit = swap_bits(core)

    def rows_of(part, rows):
        if part is opposite:
            return jnp.where(core == 1, opposite[rows, :].astype(F32), opposite_hop[rows, :].astype(F32))
        return part[rows, :].astype(F32)

    for part, k in ((own, 0), (by_far, far_bit), (by_near, near_bit), (opposite, 3)):
        ids = rows_of(part, slice(quota * size, None)).astype(jnp.int32)
        for i in range(quota):
            target, slot = ids[2 * i, 0], ids[2 * i + 1, 0]
            entry = target ^ table if relative else target
            known = first_slot[entry]
            which = jnp.where((known < 0) | (known == slot), 0, 1)
            first_slot[entry] = jnp.where(known < 0, slot, known)
            place = entry * LIST + which
            slots[place] = slot
            index_ref[k * quota + i] = place
            total[place] += rows_of(part, slice(i * size, (i + 1) * size))
    for r in range(tables):
        out, base = outs[r // CORES], r % CORES * (LIST * size + META)
        for e in range(LIST):
            out[base + e * size : base + (e + 1) * size, :] = total[r * LIST + e].astype(BF16)
        base += LIST * size
        out[base : base + META, :] = id_rows([slots[r * LIST + e] for e in range(LIST)], META)


def pool_kernel(tables, size, *refs):
    parts = refs[:tables]
    dense_ref, cot_ref, v_ref, first_ref, scaled_ref, slot_ref, hidden_ref, total = refs[tables:]
    for b in range(BAG_BLOCKS + 1):
        total[b] = jnp.zeros((size, 128), F32)
    for r in range(tables):
        part, base = parts[r], r % CORES * (LIST * size + META)
        ids = part[base + LIST * size : base + LIST * size + META, :].astype(F32).astype(jnp.int32)
        for e in range(LIST):
            slot_ref[r * LIST + e] = ids[e, 0]
            begin = base + e * size
            place = jnp.where(ids[e, 0] < 0, BAG_BLOCKS, ids[e, 0])
            total[place] += part[begin : begin + size, :].astype(F32)

    first_ref[:, :128] = dense_ref[...]
    for f in range(FEATURES):
        for s in range(SAMPLE_BLOCKS):
            columns = slice((f + 1) * 128, (f + 2) * 128)
            first_ref[s * size : (s + 1) * size, columns] = total[f * SAMPLE_BLOCKS + s].astype(BF16)
    hidden_ref[...] = dot(first_ref[...], v_ref[...]).astype(BF16)
    for f in range(FEATURES + 1):
        columns = slice(f * 128, (f + 1) * 128)
        scaled_ref[:, columns] = (cot_ref[:, columns].astype(F32) * first_ref[:, columns].astype(F32)).astype(BF16)


def blocks_kernel(group, size, slot_ref, hidden_ref, dhidden_ref, v_ref, u_ref, bias_ref, cot_ref, *outs):
    for chip, out in zip(group, outs):
        for entry in range(CORES * LIST):
            slot = jnp.maximum(slot_ref[chip * CORES * LIST + entry], 0)
            columns = block(slot // SAMPLE_BLOCKS + 1, 128)
            samples = block(slot % SAMPLE_BLOCKS, size)
            scale = dot(hidden_ref[samples, :], u_ref[:, columns]) + bias_ref[:, columns]
            grad = cot_ref[samples, columns].astype(F32) * (scale + 1.0)
            grad = grad + nt_dot(dhidden_ref[samples, :], v_ref[columns, :])
            out[entry * size : (entry + 1) * size, :] = grad.astype(BF16)


def owner_kernel(group, size, slot_ref, hidden_ref, scaled_ref, v_ref, u_ref, bias_ref, cot_ref, *outs):
    dhidden_ref = outs[-1]
    dhidden_ref[...] = nt_dot(scaled_ref[...], u_ref[...]).astype(BF16)
    blocks_kernel(group, size, slot_ref, hidden_ref, dhidden_ref, v_ref, u_ref, bias_ref, cot_ref, *outs[:-1])


def cross_kernel(first_ref, hidden_ref, u_ref, bias_ref, out_ref):
    width = first_ref.shape[1]
    step = 256
    for start in range(0, width, step):
        columns = slice(start, min(start + step, width))
        scale = dot(hidden_ref[...], u_ref[:, columns]) + bias_ref[:, columns]
        out_ref[:, columns] = (first_ref[:, columns].astype(F32) * (scale + 1.0)).astype(BF16)


def return_kernel(nodes, quota, size, tables, index_ref, *refs):
    parts, outs, staged = refs[:tables], refs[tables : tables + nodes], refs[-1]
    for r in range(tables):
        for e in range(LIST):
            begin = (r % CORES * LIST + e) * size
            staged[r * LIST + e] = parts[r][begin : begin + size, :]
    for k in range(nodes):
        for i in range(quota):
            outs[k][i * size : (i + 1) * size, :] = staged[index_ref[k * quota + i]]


def rows_kernel(nodes, quota, size, rows_ref, mult_ref, *refs):
    parts, out_ref = refs[:nodes], refs[nodes]
    node = lax.axis_index("node")
    out_ref[...] = jnp.zeros(out_ref.shape, F32)
    for k in range(nodes):
        for i in range(quota):
            tile = (node ^ k) * quota + i
            weights = mult_ref[tile].astype(F32).astype(BF16)
            rows = block(rows_ref[tile], size)
            out_ref[rows, :] += tn_dot(weights, parts[k][i * size : (i + 1) * size, :])


def xor_permute(value, axis, k):
    size = lax.axis_size(axis)
    return lax.ppermute(value, axis, [(i, i ^ k) for i in range(size)])


def exchange_chips(parts):
    arrived = list(parts)
    for k in range(1, len(parts)):
        arrived[k] = xor_permute(parts[k], "table", CORES * k)
    return arrived


def exchange_cores(parts):
    return [item for part in parts for item in (part, sibling(part))]


def exchange_whole(parts):
    height = parts[0].shape[0] // CORES
    stacked = jnp.stack(parts).reshape(len(parts) * CORES, height, parts[0].shape[1])
    moved = lax.all_to_all(stacked, "table", split_axis=0, concat_axis=0, tiled=True)
    moved = moved.reshape(len(parts), CORES * height, parts[0].shape[1])
    return [moved[r // CORES] for r in range(len(parts) * CORES)]


def permute(value, target):
    nodes, tables = lax.axis_size("node"), lax.axis_size("table")
    pairs = []
    for n in range(nodes):
        for t in range(tables):
            m, s = target(n, t)
            pairs.append((n * tables + t, m * tables + s))
    return lax.ppermute(value, ("node", "table"), pairs)


def near(value):
    return permute(value, lambda n, t: (n ^ (1 + t % 2), t))


def far(value):
    return permute(value, lambda n, t: (n ^ (2 - t % 2), t))


def across(value):
    return permute(value, lambda n, t: (n ^ 3 * (t % 2), t))


def sibling(value):
    return permute(value, lambda n, t: (n, t ^ 1))


def half_of(shard):
    half = shard.shape[0] // 2
    core = lax.axis_index("table") % 2
    return lax.dynamic_slice(shard, (core * half, 0), (half, shard.shape[1]))


def assemble(shard, first, first_other, second, second_other):
    node = lax.axis_index("node")
    core = lax.axis_index("table") % 2
    rows, width = shard.shape
    half = rows // 2
    whole = jnp.zeros((rows * lax.axis_size("node"), width), shard.dtype)
    for piece, row in (
        (shard, node * rows),
        (first, (node ^ (1 + core)) * rows),
        (first_other, (node ^ (2 - core)) * rows),
        (second, (node ^ 3) * rows + core * half),
        (second_other, (node ^ 3) * rows + (1 - core) * half),
    ):
        whole = lax.dynamic_update_slice(whole, piece, (row, 0))
    return whole


def body(emb_rows, tile_mult, tile_rows, tile_table, tile_slot, dense, cross_v, cross_u, cross_bias, cotangent):
    nodes, tables = lax.axis_size("node"), lax.axis_size("table")
    tiles, size = tile_mult.shape[0], tile_mult.shape[1]
    quota = tiles // nodes
    samples, cross = cotangent.shape
    rank = cross_v.shape[1]
    relative = tables <= 8

    part = jax.ShapeDtypeStruct((quota * size + meta_rows(quota), 128), BF16)
    hbm = pl.BlockSpec(memory_space=pltpu.HBM)
    parts = pl.pallas_call(
        functools.partial(products_kernel, quota, size),
        out_shape=[part] * 5,
        in_specs=[hbm] * 5,
        out_specs=[VMEM] * 5,
        scratch_shapes=[
            pltpu.SMEM((tiles,), jnp.int32),
            pltpu.SMEM((tiles,), jnp.int32),
            pltpu.SMEM((tiles,), jnp.int32),
            pltpu.VMEM(emb_rows.shape, BF16),
            pltpu.VMEM(tile_mult.shape, jnp.int32),
            pltpu.SemaphoreType.DMA((5,)),
        ],
        compiler_params=params(60),
        name="products",
    )(tile_rows, tile_table, tile_slot, emb_rows, tile_mult)
    first_v = near(cross_v)
    first_u = near(cross_u)
    own, far_out, opposite, hop_near, hop_opposite = parts
    parts = [
        own,
        far(far_out),
        sibling(far(sibling(hop_near))),
        across(opposite),
        sibling(across(sibling(hop_opposite))),
    ]
    chips = tables // CORES
    listed = jax.ShapeDtypeStruct((CORES * (LIST * size + META), 128), BF16)
    *lists, index = pl.pallas_call(
        functools.partial(relay_kernel, quota, size, tables, relative),
        out_shape=[listed] * chips + [jax.ShapeDtypeStruct((tiles,), jnp.int32)],
        in_specs=[VMEM] * 5,
        out_specs=[VMEM] * chips + [SMEM],
        scratch_shapes=[
            pltpu.VMEM((tables * LIST, size, 128), F32),
            pltpu.SMEM((tables,), jnp.int32),
            pltpu.SMEM((tables * LIST,), jnp.int32),
        ],
        compiler_params=params(32),
        cost_estimate=pl.CostEstimate(flops=RELAY_FLOPS, bytes_accessed=0, transcendentals=0),
        name="relay",
    )(*parts)
    half_v = half_of(first_v)
    if relative:
        half_v, lists[1] = lax.optimization_barrier((half_v, lists[1]))
    second_v = far(half_v)
    first_u, first_v, late_v, late_u, late_bias = lax.optimization_barrier(
        (first_u, first_v, cross_v, cross_u, cross_bias)
    )
    other_v = sibling(first_v)
    second_u = far(half_of(first_u))
    bias = late_bias.reshape(1, cross)
    swap_u = first_u
    if relative:
        arrived = exchange_chips(lists)
        second_v, swap_u, *arrived = lax.optimization_barrier((second_v, first_u, *arrived))
        arrived = exchange_cores(arrived)
    else:
        arrived = exchange_whole(lists)
    full_v = assemble(late_v, first_v, other_v, second_v, sibling(second_v))

    grad = jax.ShapeDtypeStruct((CORES * LIST * size, 128), BF16)
    first, scaled, slots, hidden = pl.pallas_call(
        functools.partial(pool_kernel, tables, size),
        out_shape=[
            jax.ShapeDtypeStruct((samples, cross), BF16),
            jax.ShapeDtypeStruct((samples, cross), BF16),
            jax.ShapeDtypeStruct((tables * LIST,), jnp.int32),
            jax.ShapeDtypeStruct((samples, rank), BF16),
        ],
        in_specs=[VMEM] * (tables + 3),
        out_specs=[VMEM, VMEM, SMEM, VMEM],
        scratch_shapes=[pltpu.VMEM((BAG_BLOCKS + 1, size, 128), F32)],
        compiler_params=params(24),
        name="pool",
    )(*arrived, dense, cotangent, full_v)

    if relative:
        second_u, scaled = lax.optimization_barrier((second_u, scaled))
    full_u = assemble(late_u, first_u, sibling(swap_u), second_u, sibling(second_u))

    groups = (range(chips - 1, chips), range(chips - 1))
    *far_grads, dhidden = pl.pallas_call(
        functools.partial(owner_kernel, groups[0], size),
        out_shape=[grad] * len(groups[0]) + [jax.ShapeDtypeStruct((samples, rank), BF16)],
        in_specs=[SMEM] + [VMEM] * 6,
        out_specs=[VMEM] * (len(groups[0]) + 1),
        compiler_params=params(24),
        name="owner",
    )(slots, hidden, scaled, full_v, full_u, bias, cotangent)
    near_grads = pl.pallas_call(
        functools.partial(blocks_kernel, groups[1], size),
        out_shape=[grad] * len(groups[1]),
        in_specs=[SMEM] + [VMEM] * 6,
        out_specs=[VMEM] * len(groups[1]),
        compiler_params=params(24),
        name="blocks",
    )(slots, hidden, dhidden, full_v, full_u, bias, cotangent)
    grads = [*near_grads, *far_grads]

    cross_out = pl.pallas_call(
        cross_kernel,
        out_shape=jax.ShapeDtypeStruct((samples, cross), BF16),
        in_specs=[VMEM] * 4,
        out_specs=VMEM,
        compiler_params=params(32),
        cost_estimate=pl.CostEstimate(
            flops=2 * samples * rank * cross, bytes_accessed=4 * samples * cross + 2 * rank * cross, transcendentals=0
        ),
        name="cross",
    )(first, hidden, full_u, bias)

    if relative:
        returned = exchange_chips(grads)
        returned[-1], cross_out = lax.optimization_barrier((returned[-1], cross_out))
        returned = exchange_cores(returned)
    else:
        returned = exchange_whole(grads)

    back = jax.ShapeDtypeStruct((quota * size, 128), BF16)
    backs = pl.pallas_call(
        functools.partial(return_kernel, nodes, quota, size, tables),
        out_shape=[back] * nodes,
        in_specs=[SMEM] + [VMEM] * tables,
        out_specs=[VMEM] * nodes,
        scratch_shapes=[pltpu.VMEM((tables * LIST, size, 128), BF16)],
        compiler_params=params(32),
        name="back",
    )(index, *returned)
    backs = list(backs)
    for k in range(1, nodes):
        backs[k] = xor_permute(backs[k], "node", k)

    emb_grad = pl.pallas_call(
        functools.partial(rows_kernel, nodes, quota, size),
        out_shape=jax.ShapeDtypeStruct(emb_rows.shape, F32),
        in_specs=[SMEM] + [VMEM] * (nodes + 1),
        out_specs=VMEM,
        compiler_params=params(16),
        name="rows",
    )(tile_rows, tile_mult, *backs)
    return cross_out, emb_grad


def solution(mesh):
    both = ("node", "table")
    in_specs = (
        P(both, None),
        P(both, None, None),
        P(both),
        P(both),
        P(both),
        P(both, None),
        P("node", None),
        P("node", None),
        P(),
        P(both, None),
    )
    out_specs = (P(both, None), P(both, None))
    return jax.shard_map(body, mesh=mesh, in_specs=in_specs, out_specs=out_specs, check_vma=False)
```
